32 devices in a mesh: dp: 8 (over y, x, core), tensor: 4 (over z).
Axes of the slice: x: 2, y: 2, z: 4, core: 2. Of those that a mesh axis runs over, the one named last changes fastest.
Arguments:
- inputs: bfloat16 [16, 1024, 1024], P('dp', None, 'tensor'), may hold values from -6 to 6
- segment: int32 [16, 1024], P('dp'), may hold values from 0 to 4, as said below
- cotangent: bfloat16 [16, 1024, 1024], P('dp', None, 'tensor'), may hold values from -6 to 6
- norm_gain: float32 [1024], replicated, may hold values from 0.1 to 1.9
- weight_z: bfloat16 [1024, 2048], P(None, 'tensor'), may hold values from -0.1875 to 0.1875
- weight_x: bfloat16 [1024, 2048], P(None, 'tensor'), may hold values from -0.1875 to 0.1875
- weight_bc: bfloat16 [1024, 256], replicated, may hold values from -0.1875 to 0.1875
- weight_dt: bfloat16 [1024, 32], P(None, 'tensor'), may hold values from -0.1875 to 0.1875
- conv_weight_x: float32 [4, 2048], P(None, 'tensor'), may hold values from -3 to 3
- conv_bias_x: float32 [2048], P('tensor'), may hold values from -3 to 3
- conv_weight_bc: float32 [4, 256], replicated, may hold values from -3 to 3
- conv_bias_bc: float32 [256], replicated, may hold values from -3 to 3
- step_bias: float32 [32], P('tensor'), may hold values from -6 to -2
- decay_log: float32 [32], P('tensor'), may hold values from 0 to 2.77
- skip_gain: float32 [32], P('tensor'), may hold values from 0.5 to 2
- gate_gain: float32 [2048], P('tensor'), may hold values from 0.1 to 1.9
- weight_out: bfloat16 [2048, 1024], P('tensor'), may hold values from -0.125 to 0.125
Outputs:
- output: bfloat16 [16, 1024, 1024], P('dp', None, 'tensor')
- input_grad: float32 [16, 1024, 1024], P('dp', None, 'tensor')
- norm_gain_grad: float32 [1024], P('tensor')
- weight_z_grad: float32 [1024, 2048], P('dp', 'tensor')
- weight_x_grad: float32 [1024, 2048], P('dp', 'tensor')
- weight_bc_grad: float32 [1024, 256], P('dp')
- weight_dt_grad: float32 [1024, 32], P('dp', 'tensor')
- conv_weight_x_grad: float32 [4, 2048], P(None, 'tensor')
- conv_bias_x_grad: float32 [2048], P('tensor')
- conv_weight_bc_grad: float32 [4, 256], replicated
- conv_bias_bc_grad: float32 [256], replicated
- step_bias_grad: float32 [32], P('tensor')
- decay_log_grad: float32 [32], P('tensor')
- skip_gain_grad: float32 [32], P('tensor')
- gate_gain_grad: float32 [2048], P('tensor')
- weight_out_grad: float32 [2048, 1024], P('tensor', 'dp')
The draws below stay inside these ranges and needn't reach their ends.
Inputs may be any that keep to these rules, and one draw needn't show every extreme that they name: `segment`: segment numbers start at 0 in each sequence and never fall along it; a new number starts a new document, where the scan state and the convolution restart. Each sequence holds one document of exactly 800 tokens, at its start or at its end; the inner documents have 60 to 800 tokens, the one at the other end may be shorter.
All inputs are finite; a program needn't handle non-finite values.
Results may differ from the reference program's by a relative error of at most 0.008.
Values may be sent and summed in bfloat16 or wider, within the bound.
No kernel may reach another device: no remote copies, remote signals or barrier semaphores. Data moves between devices by JAX's collectives and lax.ppermute only.
A program may use at most 192 MiB of HBM per device.

```python
import jax
import jax.numpy as jnp
from jax import lax

D = 1024
HEADS = 32
STATE = 128
CONV = 4
SPAN = 256
LEN = 1024
SEQ_MB = 1
INNER = 2048
DOC_MAX = 800
DOC_MIN = 60
SEQS = 16


def draw_segment(key, part):
    key_len = jax.random.fold_in(key, 11)
    key_flip = jax.random.fold_in(key, 23)
    doc_count = LEN // DOC_MIN + 1
    lengths = jax.random.randint(key_len, (SEQS, doc_count), DOC_MIN, DOC_MAX + 1)
    rows = jnp.arange(SEQS)[:, None]
    lengths = jnp.where(rows == 0, DOC_MIN, lengths)
    lengths = lengths.at[:, 0].set(DOC_MAX)
    ends = jnp.cumsum(lengths, axis=1)
    places = jnp.arange(LEN)
    numbers = jnp.sum((ends[:, None, :] <= places[None, :, None]).astype(jnp.int32), axis=2)
    reversed_order = jax.random.randint(key_flip, (SEQS, 1), 0, 2)
    mirrored = numbers[:, -1:] - numbers[:, ::-1]
    return jnp.where(reversed_order == 1, mirrored, numbers).astype(jnp.int32)


def level_of(stream_key, extent, shards, low, high):
    def one(position, shards_of):
        draws = jax.random.uniform(jax.random.fold_in(jax.random.fold_in(stream_key, 6), position), (shards_of,), jnp.float32, low / len(shards), high / len(shards))
        return jnp.repeat(jnp.exp(draws), extent[position] // shards_of).reshape((-1,) + (1,) * (len(extent) - position - 1))

    factor_of = one(*shards[0])
    for cut in shards[1:]:
        factor_of = factor_of * one(*cut)
    return factor_of


def scatter_about(key, extent, deviation, bound, cuts=(), held_as=jnp.bfloat16):
    entries = deviation * jax.random.normal(key, extent, jnp.float32)
    if cuts:
        entries = entries * level_of(key, extent, cuts, -0.22, 0.18)
    return jnp.clip(entries, -bound, bound).astype(held_as)


def setup_inputs(seed: int = 0) -> dict:
    splits = jax.random.split(jax.random.key(seed), 18)
    return {
        "inputs": scatter_about(splits[0], (SEQS, LEN, D), 1.0, 6.0, ((0, 8), (2, 4))),
        "segment": draw_segment(jax.random.fold_in(splits[17], 71), 0),
        "cotangent": scatter_about(splits[2], (SEQS, LEN, D), 1.0, 6.0, ((0, 8), (2, 4))),
        "norm_gain": jnp.clip(1.0 + 0.18 * jax.random.normal(splits[3], (D,), jnp.float32), 0.1, 1.9),
        "weight_z": scatter_about(splits[4], (D, INNER), D ** -0.5, 0.1875, ((1, 4),)),
        "weight_x": scatter_about(splits[5], (D, INNER), D ** -0.5, 0.1875, ((1, 4),)),
        "weight_bc": scatter_about(splits[6], (D, 2 * STATE), D ** -0.5, 0.1875),
        "weight_dt": scatter_about(splits[7], (D, HEADS), D ** -0.5, 0.1875, ((1, 4),)),
        "conv_weight_x": scatter_about(splits[8], (CONV, INNER), CONV ** -0.5, 3.0, ((1, 4),), jnp.float32),
        "conv_bias_x": scatter_about(splits[9], (INNER,), 0.5, 3.0, ((0, 4),), jnp.float32),
        "conv_weight_bc": scatter_about(splits[10], (CONV, 2 * STATE), CONV ** -0.5, 3.0, (), jnp.float32),
        "conv_bias_bc": scatter_about(splits[11], (2 * STATE,), 0.5, 3.0, (), jnp.float32),
        "step_bias": jnp.clip(-6.0 + 4.0 * jax.random.uniform(splits[12], (HEADS,), jnp.float32) ** level_of(splits[12], (HEADS,), ((0, 4),), -0.2, 0.2), -6.0, -2.0),
        "decay_log": jnp.clip(2.77 * jax.random.uniform(splits[13], (HEADS,), jnp.float32) ** level_of(splits[13], (HEADS,), ((0, 4),), -0.2, 0.2), 0.0, 2.77),
        "skip_gain": jnp.clip(0.5 + 1.5 * jax.random.uniform(splits[14], (HEADS,), jnp.float32) ** level_of(splits[14], (HEADS,), ((0, 4),), -0.2, 0.2), 0.5, 2.0),
        "gate_gain": jnp.clip(1.0 + 0.18 * jax.random.normal(splits[15], (INNER,), jnp.float32), 0.1, 1.9),
        "weight_out": scatter_about(splits[16], (INNER, D), INNER ** -0.5, 0.125, ((0, 4),)),
    }


@jax.custom_vjp
def low(v):
    return lax.optimization_barrier(v.astype(jnp.bfloat16)).astype(jnp.float32)

@jax.custom_vjp
def low_back(v):
    return v

def low_keep(v):
    return (low(v), None)

def low_pass(kept, grad):
    return (grad,)

def back_keep(v):
    return (v, None)

def back_low(kept, grad):
    return (low(grad),)
low.defvjp(low_keep, low_pass)
low_back.defvjp(back_keep, back_low)
eps = 1e-05
exact_precision = lax.Precision.HIGHEST

def causal_conv(values, weights, biases, segment):
    taps = weights.shape[0]
    total = biases + weights[taps - 1] * values
    for offset in range(1, taps):
        moved = jnp.pad(values, ((0, 0), (offset, 0), (0, 0)))[:, :-offset]
        earlier = jnp.pad(segment, ((0, 0), (offset, 0)), constant_values=-1)[:, :-offset]
        same_doc = (earlier == segment).astype(values.dtype)[..., None]
        total = total + weights[taps - 1 - offset] * moved * same_doc
    return total

def ssd_scan(values, decays, deltas, b_matrix, c_matrix, segment, block_len):
    seq_count, length, head_count, head_size = values.shape
    block_count = length // block_len

    def to_blocks(source):
        shaped = source.reshape((seq_count, block_count, block_len) + source.shape[2:])
        return jnp.moveaxis(shaped, 1, 0)
    pieces = tuple((to_blocks(source) for source in (values, decays, deltas, b_matrix, c_matrix, segment)))
    state_init = jnp.zeros((seq_count, head_count, b_matrix.shape[-1], head_size), values.dtype)
    prev_init = jnp.full((seq_count,), -1, jnp.int32)
    lower_tri = jnp.arange(block_len)[:, None] >= jnp.arange(block_len)[None, :]

    def advance(carried_in, block_in):
        prior_state, previous = carried_in
        value_blk, decay_blk, delta_blk, b_blk, c_blk, seg_blk = block_in
        cumulative = jnp.cumsum(decay_blk, axis=1)
        allowed = (seg_blk[:, :, None] == seg_blk[:, None, :]) & lower_tri[None]
        masking = allowed.astype(values.dtype)[..., None]
        spread = cumulative[:, :, None, :] - cumulative[:, None, :, :]
        kernel = jnp.exp(jnp.where(allowed[..., None], spread, 0.0)) * masking
        scores = jnp.einsum('stn,sun->stu', c_blk, b_blk, precision=exact_precision)
        mixing = scores[..., None] * kernel * delta_blk[:, None, :, :]
        inside = jnp.einsum('stuh,suhp->sthp', mixing, value_blk, precision=exact_precision)
        final_seg = seg_blk[:, -1]
        same_end = (seg_blk == final_seg[:, None]).astype(values.dtype)[..., None]
        tail_weight = jnp.exp(cumulative[:, -1:, :] - cumulative) * same_end * delta_blk
        local_state = jnp.einsum('sun,suhp->shnp', b_blk, tail_weight[..., None] * value_blk, precision=exact_precision)
        entering = jnp.exp(cumulative) * (seg_blk == previous[:, None]).astype(values.dtype)[..., None]
        outside = jnp.einsum('stn,shnp->sthp', c_blk, prior_state, precision=exact_precision) * entering[..., None]
        carried = jnp.exp(cumulative[:, -1, :]) * (final_seg == previous).astype(values.dtype)[:, None]
        new_state = carried[:, :, None, None] * prior_state + local_state
        return ((new_state, final_seg), inside + outside)
    _, results = lax.scan(jax.checkpoint(advance), (state_init, prev_init), pieces)
    return jnp.moveaxis(results, 0, 1).reshape(seq_count, length, head_count, head_size)

def mixer(gate_pre, value_pre, bc_pre, delta_pre, params, segment):
    conv_weight_x, conv_bias_x, conv_weight_bc, conv_bias_bc, step_bias, decay_log, skip_gain = params
    conv_value = jax.nn.silu(causal_conv(value_pre, conv_weight_x, conv_bias_x, segment))
    conv_bc = jax.nn.silu(causal_conv(bc_pre, conv_weight_bc, conv_bias_bc, segment))
    state_size = conv_bc.shape[-1] // 2
    deltas = jax.nn.softplus(delta_pre + step_bias)
    decays = -deltas * jnp.exp(decay_log)
    seq_count, length, head_count = deltas.shape
    values = conv_value.reshape(seq_count, length, head_count, -1)
    scan_result = ssd_scan(values, decays, deltas, conv_bc[..., :state_size], conv_bc[..., state_size:], segment, SPAN)
    scan_result = scan_result + skip_gain[:, None] * values
    return scan_result.reshape(gate_pre.shape) * jax.nn.silu(gate_pre)

def project(left_operand, right_operand):
    return jnp.einsum('ofp,pv->ofv', left_operand, right_operand, precision=exact_precision)

def layer(residual, floats, segment):
    norm_gain, weight_z, weight_x, weight_bc, weight_dt, conv_weight_x, conv_bias_x, conv_weight_bc, conv_bias_bc, step_bias, decay_log, skip_gain, gate_gain, weight_out = floats
    scale_in = lax.rsqrt(lax.optimization_barrier(jnp.mean(residual * residual, axis=-1, keepdims=True)) + eps)
    normed = low(residual * scale_in * norm_gain)
    gate_pre = low_back(project(normed, weight_z))
    value_pre = low_back(project(normed, weight_x))
    bc_pre = low_back(project(normed, weight_bc))
    delta_pre = low_back(project(normed, weight_dt))
    params = (conv_weight_x, conv_bias_x, conv_weight_bc, conv_bias_bc, step_bias, decay_log, skip_gain)
    gated_out = mixer(gate_pre, value_pre, bc_pre, delta_pre, params, segment)
    scale_gate = lax.rsqrt(lax.optimization_barrier(jnp.mean(gated_out * gated_out, axis=-1, keepdims=True)) + eps)
    mixer_output = low(gated_out * scale_gate * gate_gain)
    return residual + project(mixer_output, weight_out)

def add_tree(left_operand, right_operand):
    return jax.tree.map(jnp.add, left_operand, right_operand)

def reference(inputs, segment, cotangent, norm_gain, weight_z, weight_x, weight_bc, weight_dt, conv_weight_x, conv_bias_x, conv_weight_bc, conv_bias_bc, step_bias, decay_log, skip_gain, gate_gain, weight_out):
    floats = tuple((item.astype(jnp.float32) for item in (norm_gain, weight_z, weight_x, weight_bc, weight_dt, conv_weight_x, conv_bias_x, conv_weight_bc, conv_bias_bc, step_bias, decay_log, skip_gain, gate_gain, weight_out)))
    group_count = inputs.shape[0] // SEQ_MB

    def regroup(source):
        return source.reshape((group_count, SEQ_MB) + source.shape[1:])

    def one_group(totals, block_in):
        resid_blk, seg_blk, cot_blk = block_in

        def forward(residual, weights_all):
            return layer(residual, weights_all, seg_blk)
        result, pullback = jax.vjp(forward, resid_blk.astype(jnp.float32), floats)
        grad_in, grad_params = pullback(cot_blk.astype(jnp.float32))
        return (add_tree(totals, grad_params), (result.astype(jnp.bfloat16), grad_in))
    start_totals = jax.tree.map(jnp.zeros_like, floats)
    totals, (results, grads_in) = lax.scan(one_group, start_totals, (regroup(inputs), regroup(segment), regroup(cotangent)))
    output = results.reshape(inputs.shape)
    input_grad = grads_in.reshape(inputs.shape)
    return (output, input_grad, totals[0], totals[1], totals[2], totals[3], totals[4], totals[5], totals[6], totals[7], totals[8], totals[9], totals[10], totals[11], totals[12], totals[13])
```

```python
import functools

import jax
import jax.numpy as jnp
from jax import lax
from jax.experimental import pallas as pl
from jax.experimental.layout import Layout, with_layout_constraint
from jax.experimental.pallas import tpu as pltpu
from jax.sharding import Mesh
from jax.sharding import PartitionSpec as P

SPAN = 256
HEAD = 64
LANES = 128
LOG2E = 1.4426950408889634
FAR = -1e30
bf16 = jnp.bfloat16
f32 = jnp.float32


def dot_nn(a, b):
    return lax.dot_general(a, b, (((1,), (0,)), ((), ())), preferred_element_type=f32)


def dot_nt(a, b):
    return lax.dot_general(a, b, (((1,), (1,)), ((), ())), preferred_element_type=f32)


def dot_tn(a, b):
    return lax.dot_general(a, b, (((0,), (0,)), ((), ())), preferred_element_type=f32)


def split_dot(a, b, flip=False):
    one = a.astype(bf16)
    two = (a - one.astype(f32)).astype(bf16)
    if flip:
        return dot_nn(b, one) + dot_nn(b, two)
    return dot_nn(one, b) + dot_nn(two, b)


def conv_terms(scr, block, halo, masks):
    span = block.shape[0]
    scr[0:8, :] = halo
    scr[8 : 8 + span, :] = block
    return [block] + [scr[8 - k : 8 - k + span, :] * masks(1 + k) for k in (1, 2, 3)]


def conv_sum(terms, weights, bias):
    total = bias + weights[3:4] * terms[0]
    for k in (1, 2, 3):
        total = total + weights[3 - k : 4 - k] * terms[k]
    return total


def sigmoid(v):
    return 0.5 + 0.5 * jnp.tanh(0.5 * v)


def lanes_of(columns, pair, low):
    return jnp.where(low, columns[:, 2 * pair : 2 * pair + 1], columns[:, 2 * pair + 1 : 2 * pair + 2])


def steps_of(pre, rate, lower, upper):
    dt = jnp.maximum(pre, 0.0) + jnp.log1p(jnp.exp(-jnp.abs(pre)))
    decay = dt * (rate * LOG2E)
    cum, cum_t = None, None
    for _ in range(3):
        part = decay.astype(bf16)
        decay = decay - part.astype(f32)
        one, two = dot_nn(lower, part), dot_tn(part, upper)
        cum, cum_t = (one, two) if cum is None else (cum + one, cum_t + two)
    return dt, cum, cum_t


def forward_kernel(
    v_ref, vh_ref, bc_ref, bch_ref, pre_ref, rate_ref, aux_ref, segc_ref, segr_ref,
    cw_ref, cb_ref, cwb_ref, cbb_ref, skip_ref,
    y_ref, hprev_ref, steps_ref, cumt_ref, state, scr, scrb, far_ref, mask_ref,
):
    span = v_ref.shape[0]
    pairs = v_ref.shape[1] // LANES
    n = bc_ref.shape[1] // 2

    @pl.when(pl.program_id(0) == 0)
    def _():
        state[...] = jnp.zeros_like(state)

    aux = aux_ref[...]
    for i in range(5):
        mask_ref[i] = jnp.broadcast_to(aux[:, i : i + 1], (span, LANES))
    bc_act = conv_sum(conv_terms(scrb, bc_ref[...], bch_ref[...], lambda i: aux[:, i : i + 1]), cwb_ref[...], cbb_ref[...])
    bc_act = bc_act * sigmoid(bc_act)
    b_mat = bc_act[:, :n].astype(bf16)
    c_mat = bc_act[:, n:].astype(bf16)
    scores = dot_nt(c_mat, b_mat)
    later = lax.broadcasted_iota(jnp.int32, (span, span), 0)
    earlier = lax.broadcasted_iota(jnp.int32, (span, span), 1)
    lower = (later >= earlier).astype(f32).astype(bf16)
    upper = (earlier >= later).astype(f32).astype(bf16)
    dt, cum, cum_t = steps_of(pre_ref[...], rate_ref[...], lower, upper)
    far_ref[...] = jnp.where((segc_ref[...] == segr_ref[...]) & (later >= earlier), 0.0, FAR)
    low = lax.broadcasted_iota(jnp.int32, (1, LANES), 1) < HEAD
    steps_ref[...] = jnp.concatenate([dt, cum, sigmoid(pre_ref[...])], axis=1)
    cumt_ref[...] = cum_t
    half = span // 2
    for p in range(pairs):
        sl = slice(p * LANES, (p + 1) * LANES)
        act = conv_sum(conv_terms(scr, v_ref[:, sl], vh_ref[:, sl], lambda i: mask_ref[i]), cw_ref[:, sl], cb_ref[:, sl])
        x = act * sigmoid(act)
        v = (x * lanes_of(dt, p, low)).astype(bf16)
        inside = None
        for e in (0, 1):
            h = 2 * p + e
            mine = jnp.where(low if e == 0 else ~low, v, jnp.zeros_like(v))
            part = []
            for rows, columns in ((slice(0, half), slice(0, half)), (slice(half, span), slice(0, span))):
                spread = (cum[rows, h : h + 1] - cum_t[h : h + 1, columns]) + far_ref[rows, columns]
                mixing = (scores[rows, columns] * jnp.exp2(spread)).astype(bf16)
                part.append(dot_nn(mixing, mine[columns]))
            part = jnp.concatenate(part, axis=0)
            inside = part if inside is None else inside + part
        wide_cum = lanes_of(cum, p, low)
        enter = jnp.exp2(wide_cum) * mask_ref[0]
        tail = jnp.exp2(wide_cum[span - 1 : span] - wide_cum) * mask_ref[1]
        prior = state[:, sl]
        low_prior = prior.astype(bf16)
        hprev_ref[0, :, sl] = low_prior
        outside = dot_nn(c_mat, low_prior) * enter
        y_ref[:, sl] = inside + outside + skip_ref[:, sl] * x
        weighted = (tail * v.astype(f32)).astype(bf16)
        state[:, sl] = enter[span - 1 : span] * prior + dot_tn(b_mat, weighted)


def backward_kernel(
    first, more, shares, where_ref,
    v_ref, vh_ref, bc_ref, bch_ref, steps_ref, rate_ref, aux_ref, segc_ref, segr_ref,
    cw_ref, cb_ref, cwb_ref, cbb_ref, skip_ref, cumt_ref, y_ref, dy_ref, hprev_ref, *rest,
):
    if more:
        before_refs, rest = rest[:shares], rest[shares:]
    dbc_refs, rest = rest[:shares], rest[shares:]
    (
        dv_ref, ddelta_ref, gx_ref, gbc_ref, gh_ref,
        dstate, after, afterb, scr, scrb, far_ref, dscore, dot_y, dot_x, last, tailed, entered, mask_ref,
    ) = rest
    span = v_ref.shape[0]
    channels = v_ref.shape[1]
    pairs = channels // LANES
    heads = channels // HEAD
    everyone = steps_ref.shape[1] // 3
    dt, cum, slope_dt = (steps_ref[:, i * everyone + first : i * everyone + first + heads] for i in range(3))
    rate = rate_ref[:, first : first + heads]
    half = span // 2
    n = bc_ref.shape[1] // 2

    @pl.when(pl.program_id(0) == 0)
    def _():
        for ref in (dstate, after, afterb, gx_ref, gbc_ref, gh_ref):
            ref[...] = jnp.zeros_like(ref)

    aux = aux_ref[...]
    for i in range(8):
        mask_ref[i] = jnp.broadcast_to(aux[:, i : i + 1], (span, LANES))
    terms_bc = conv_terms(scrb, bc_ref[...], bch_ref[...], lambda i: aux[:, i : i + 1])
    act_bc = conv_sum(terms_bc, cwb_ref[...], cbb_ref[...])
    sig_bc = sigmoid(act_bc)
    bc_act = act_bc * sig_bc
    b_mat = bc_act[:, :n].astype(bf16)
    c_mat = bc_act[:, n:].astype(bf16)
    scores = dot_nt(b_mat, c_mat)
    earlier = lax.broadcasted_iota(jnp.int32, (span, span), 0)
    later = lax.broadcasted_iota(jnp.int32, (span, span), 1)
    far_ref[...] = jnp.where((segc_ref[...] == segr_ref[...]) & (later >= earlier), 0.0, FAR)
    low = lax.broadcasted_iota(jnp.int32, (1, LANES), 1) < HEAD
    upper = (later >= earlier).astype(f32).astype(bf16)
    dscore[...] = jnp.zeros_like(dscore)

    def rows_of(value):
        return jnp.sum(value, axis=0, keepdims=True)

    for p in range(pairs):
        sl = slice(p * LANES, (p + 1) * LANES)
        terms = conv_terms(scr, v_ref[:, sl], vh_ref[:, sl], lambda i: mask_ref[i])
        act = conv_sum(terms, cw_ref[:, sl], cb_ref[:, sl])
        sig = sigmoid(act)
        x = act * sig
        dt_lanes = lanes_of(dt, p, low)
        v = (x * dt_lanes).astype(bf16)
        v_wide = v.astype(f32)
        dy = dy_ref[:, sl]
        dy_wide = dy.astype(f32)
        d_inside = None
        for e in (0, 1):
            h = 2 * p + e
            mask = low if e == 0 else ~low
            mine = jnp.where(mask, dy, jnp.zeros_like(dy))
            part = []
            for rows, columns in ((slice(0, half), slice(0, span)), (slice(half, span), slice(half, span))):
                spread = (cumt_ref[first + h : first + h + 1, columns] - cum[rows, h : h + 1]) + far_ref[rows, columns]
                kernel = jnp.exp2(spread)
                mixing = (scores[rows, columns] * kernel).astype(bf16)
                part.append(dot_nn(mixing, mine[columns]))
                dscore[rows, columns] += dot_nt(v[rows], mine[columns]) * kernel
            part = jnp.concatenate(part, axis=0)
            d_inside = part if d_inside is None else d_inside + part
        wide_cum = lanes_of(cum, p, low)
        enter = jnp.exp2(wide_cum) * mask_ref[0]
        tail = jnp.exp2(wide_cum[span - 1 : span] - wide_cum) * mask_ref[1]
        d_new = dstate[:, sl]
        low_new = d_new.astype(bf16)
        d_outer = dot_nn(b_mat, low_new) * tail
        dval = d_inside + d_outer
        skip = skip_ref[:, sl]
        dot_y[:, sl] = dy_wide * (y_ref[:, sl] - skip * x) - v_wide * dval
        dot_x[:, sl] = x * dval
        entering = (enter * dy_wide).astype(bf16)
        entered[:, sl] = entering
        tailed[:, sl] = (tail * v_wide).astype(bf16)
        prior = hprev_ref[0, :, sl]
        carried = enter[span - 1 : span]
        last[:, sl] = rows_of(v_wide * d_outer) + carried * rows_of(prior.astype(f32) * d_new)
        dx = dt_lanes * dval + skip * dy_wide
        dconv = dx * (sig * (1.0 + act * (1.0 - sig)))
        scr[0:span, :] = dconv
        scr[span : span + 8, :] = after[:, sl]
        d_pre = cw_ref[3:4, sl] * dconv
        for k in (1, 2, 3):
            d_pre = d_pre + cw_ref[3 - k : 4 - k, sl] * (scr[k : k + span, :] * mask_ref[4 + k])
        dv_ref[:, sl] = d_pre.astype(bf16)
        after[:, sl] = dconv[0:8]
        for k in (0, 1, 2, 3):
            gx_ref[3 - k : 4 - k, sl] += rows_of(dconv * terms[k])
        gx_ref[4:5, sl] += rows_of(dconv)
        gx_ref[5:6, sl] += rows_of(dy_wide * x)

    ds = dscore[...].astype(bf16)
    d_b = dot_nn(ds, c_mat) + dot_nt(tailed[...], dstate[...].astype(bf16))
    d_c = dot_tn(ds, b_mat) + dot_nt(entered[...], hprev_ref[0])
    slope = sig_bc * (1.0 + act_bc * (1.0 - sig_bc))
    dconv_bc = jnp.concatenate([d_b, d_c], axis=1) * slope
    scrb[0:span, :] = dconv_bc
    scrb[span : span + 8, :] = afterb[...]
    d_pre = cwb_ref[3:4] * dconv_bc
    for k in (1, 2, 3):
        d_pre = d_pre + cwb_ref[3 - k : 4 - k] * (scrb[k : k + span, :] * aux[:, 4 + k : 5 + k])
    cut = 2 * n // shares
    pieces = [d_pre[:, s * cut : (s + 1) * cut] for s in range(shares)]
    own = jnp.full((span, cut), where_ref[0], jnp.int32)
    bit = 1
    while bit < shares:
        pieces = [jnp.where((own & bit) != 0, pieces[s ^ bit], pieces[s]) for s in range(shares)]
        bit *= 2
    for e in range(shares):
        dbc_refs[e][...] = pieces[e] + before_refs[e][...] if more else pieces[e]
    afterb[...] = dconv_bc[0:8]
    for k in (0, 1, 2, 3):
        gbc_ref[3 - k : 4 - k] += rows_of(dconv_bc * terms_bc[k])
    gbc_ref[4:5] += rows_of(dconv_bc)

    for p in range(pairs):
        sl = slice(p * LANES, (p + 1) * LANES)
        carried = jnp.exp2(lanes_of(cum[span - 1 : span], p, low)) * aux[span - 1 : span, 0:1]
        dstate[:, sl] = carried * dstate[:, sl] + dot_tn(c_mat, entered[:, sl])

    place = lax.broadcasted_iota(jnp.int32, (channels, heads), 0) // HEAD
    head = lax.broadcasted_iota(jnp.int32, (channels, heads), 1)
    select = (place == head).astype(bf16)
    d_cum = split_dot(dot_y[...], select)
    final = split_dot(jnp.broadcast_to(last[...], (8, channels)), select)[0:1]
    row = lax.broadcasted_iota(jnp.int32, (span, heads), 0)
    d_cum = d_cum + jnp.where(row == span - 1, final, 0.0)
    d_decay = split_dot(d_cum, upper, flip=True)
    d_dt = split_dot(dot_x[...], select) + d_decay * rate
    d_delta = d_dt * slope_dt
    ddelta_ref[...] = d_delta
    gh_ref[0:1] += rows_of(d_delta)
    gh_ref[1:2] += rows_of(d_decay * dt * rate)


def scan_specs(common, width, column, reverse):
    length, channels = common[0].shape
    wide, heads = common[1].shape[1], common[2].shape[1]
    blocks = length // SPAN
    tall = SPAN // 8

    def at(b):
        return blocks - 1 - b if reverse else b

    def rows(size, at_column=0):
        return pl.BlockSpec((SPAN, size), lambda b, *_: (at(b), at_column))

    def halo(size, at_column=0):
        return pl.BlockSpec((8, size), lambda b, *_: (jnp.maximum(at(b) * tall - 1, 0), at_column))

    def whole(shape, at_column=0):
        return pl.BlockSpec(shape, lambda b, *_: (0, at_column))

    states = pl.BlockSpec((1, wide // 2, width), lambda b, *_: (at(b), 0, column))
    ins = [
        rows(width, column), halo(width, column), rows(wide), halo(wide), rows(heads), whole((1, heads)), rows(8), rows(1),
        pl.BlockSpec((1, SPAN), lambda b, *_: (0, at(b))),
        whole((4, width), column), whole((1, width), column), whole((4, wide)), whole((1, wide)),
        whole((1, width), column),
    ]
    return blocks, rows, whole, states, ins


def forward_scan(common):
    v_pre, bc_pre, pre = common[:3]
    length, channels = v_pre.shape
    wide, heads = bc_pre.shape[1], pre.shape[1]
    blocks, rows, whole, states, ins = scan_specs(common, channels, 0, False)
    return pl.pallas_call(
        forward_kernel,
        grid=(blocks,),
        in_specs=ins,
        out_specs=[rows(channels), states, rows(3 * heads), pl.BlockSpec((heads, SPAN), lambda b: (0, b))],
        out_shape=[
            jax.ShapeDtypeStruct((length, channels), f32),
            jax.ShapeDtypeStruct((blocks, wide // 2, channels), bf16),
            jax.ShapeDtypeStruct((length, 3 * heads), f32), jax.ShapeDtypeStruct((heads, length), f32),
        ],
        scratch_shapes=[
            pltpu.VMEM((wide // 2, channels), f32), pltpu.VMEM((SPAN + 8, LANES), f32),
            pltpu.VMEM((SPAN + 8, wide), f32), pltpu.VMEM((SPAN, SPAN), f32), pltpu.VMEM((5, SPAN, LANES), f32),
        ],
        compiler_params=pltpu.CompilerParams(vmem_limit_bytes=56 * 2**20),
        cost_estimate=pl.CostEstimate(flops=channels * length, bytes_accessed=channels * length, transcendentals=0),
    )(v_pre, v_pre, bc_pre, bc_pre, *common[2:])


def backward_scan(common, half, shares, where, steps, cum_t, y, dy, hprev, before=()):
    v_pre, bc_pre, pre = common[:3]
    length, channels = v_pre.shape[0], v_pre.shape[1] // 2
    wide, heads = bc_pre.shape[1], pre.shape[1] // 2
    blocks, rows, whole, states, ins = scan_specs(common, channels, half, True)
    split = rows(wide // shares)
    ins[4] = rows(steps.shape[1])
    sums = pl.BlockSpec((2 * heads, SPAN), lambda b, *_: (0, blocks - 1 - b))
    out = pl.pallas_call(
        functools.partial(backward_kernel, half * heads, bool(before), shares),
        grid_spec=pltpu.PrefetchScalarGridSpec(
            num_scalar_prefetch=1,
            grid=(blocks,),
            in_specs=ins + [sums, rows(channels, half), rows(channels, half), states] + [split] * len(before),
            out_specs=[split] * shares
            + [rows(channels), rows(heads), whole((8, channels)), whole((8, wide)), whole((8, heads))],
            scratch_shapes=[
                pltpu.VMEM((wide // 2, channels), f32), pltpu.VMEM((8, channels), f32), pltpu.VMEM((8, wide), f32),
                pltpu.VMEM((SPAN + 8, LANES), f32), pltpu.VMEM((SPAN + 8, wide), f32), pltpu.VMEM((SPAN, SPAN), f32),
                pltpu.VMEM((SPAN, SPAN), f32), pltpu.VMEM((SPAN, channels), f32), pltpu.VMEM((SPAN, channels), f32),
                pltpu.VMEM((1, channels), f32), pltpu.VMEM((SPAN, channels), bf16), pltpu.VMEM((SPAN, channels), bf16),
                pltpu.VMEM((8, SPAN, LANES), f32),
            ],
        ),
        out_shape=[jax.ShapeDtypeStruct((length, wide // shares), f32)] * shares
        + [
            jax.ShapeDtypeStruct((length, channels), bf16), jax.ShapeDtypeStruct((length, heads), f32),
            jax.ShapeDtypeStruct((8, channels), f32), jax.ShapeDtypeStruct((8, wide), f32),
            jax.ShapeDtypeStruct((8, heads), f32),
        ],
        compiler_params=pltpu.CompilerParams(vmem_limit_bytes=56 * 2**20),
        cost_estimate=pl.CostEstimate(flops=channels * length, bytes_accessed=channels * length, transcendentals=0),
    )(where, v_pre, v_pre, bc_pre, bc_pre, steps, *common[3:], cum_t, y, dy, hprev, *before)
    return tuple(out[:shares]), *out[shares:]


def assemble(moves, index, sources, shape):
    def kernel(index_ref, *refs):
        out_ref = refs[-1]
        at = index_ref[0]
        for source, lead, rows, base, stride, offset, columns in moves:
            start = pl.multiple_of(base + (at ^ offset) * stride, stride)
            out_ref[pl.ds(start, rows.stop - rows.start), columns] = refs[source][(*lead, rows, slice(None))]

    return pl.pallas_call(
        kernel,
        grid_spec=pltpu.PrefetchScalarGridSpec(
            num_scalar_prefetch=1,
            grid=(1,),
            in_specs=[pl.BlockSpec(v.shape, lambda i, s, rank=v.ndim: (0,) * rank) for v in sources],
            out_specs=pl.BlockSpec(shape, lambda i, s: (0, 0)),
        ),
        out_shape=jax.ShapeDtypeStruct(shape, bf16),
        compiler_params=pltpu.CompilerParams(vmem_limit_bytes=10 * 2**20),
        cost_estimate=pl.CostEstimate(flops=0, bytes_accessed=4 * shape[0] * shape[1], transcendentals=0),
    )(index.reshape(1), *sources)


def rows_in_order(shares, blocks):
    each = blocks // shares

    def at(i, where_ref):
        return (where_ref[0] ^ (shares - 1 - i // each)) * each + i % each

    return each, at


def pick_part(shares, parts, cot):
    each = pl.num_programs(0) // shares
    for e in range(shares):
        @pl.when(pl.program_id(0) // each == shares - 1 - e)
        def _(e=e):
            cot[...] = parts[e][...]


def gate_kernel(shares, where_ref, normed_ref, wz_ref, y_ref, wo_ref, gain_ref, *refs):
    parts, (stats_ref, sent_ref, kept_ref, cot) = refs[:shares], refs[shares:]
    span, model = cot.shape
    pick_part(shares, parts, cot)
    half = model // 2
    sent_ref[...] = cot[:, pl.ds(pl.multiple_of((1 - where_ref[1]) * half, half), half)].T
    kept_ref[...] = cot[:, pl.ds(pl.multiple_of(where_ref[1] * half, half), half)].T
    gate = dot_nn(normed_ref[...], wz_ref[...])
    d_mixed = dot_nt(cot[...], wo_ref[...])
    gated = y_ref[...] * (gate * sigmoid(gate))
    squares = jnp.sum(gated * gated, axis=1, keepdims=True)
    product = jnp.sum(d_mixed * gain_ref[...] * gated, axis=1, keepdims=True)
    lane = lax.broadcasted_iota(jnp.int32, (span, LANES), 1)
    both = jnp.where(lane == 0, squares, jnp.where(lane == 1, product, 0.0))
    stats_ref[...] = both.T[0:8]


def norm_kernel(
    shares, inner, where_ref, normed_ref, wz_ref, y_ref, wo_ref, gain_ref, stats_ref, *refs
):
    parts, refs = refs[:shares], refs[shares:]
    mixed_ref, dy_ref, dgate_ref, ggain_ref, sent_ref, kept_ref, cot, gate_ref, dmix_ref = refs

    @pl.when(pl.program_id(0) == 0)
    def _():
        ggain_ref[...] = jnp.zeros_like(ggain_ref)

    pick_part(shares, parts, cot)
    gate_ref[...] = dot_nn(normed_ref[...], wz_ref[...])
    dmix_ref[...] = dot_nt(cot[...], wo_ref[...])
    stats = jnp.concatenate([stats_ref[...]] + [jnp.zeros((LANES - 8, stats_ref.shape[1]), f32)], axis=0).T
    scale = lax.rsqrt(stats[:, 0:1] * (1.0 / inner) + 1e-05)
    factor = scale * scale * scale * (stats[:, 1:2] * (1.0 / inner))
    for at in range(0, y_ref.shape[1], LANES):
        sl = slice(at, at + LANES)
        y, gate, gain = y_ref[:, sl], gate_ref[:, sl], gain_ref[:, sl]
        sig = sigmoid(gate)
        silu = gate * sig
        gated = y * silu
        scaled = dmix_ref[:, sl] * scale
        mixed_ref[:, sl] = (gated * scale * gain).astype(bf16)
        d_gated = scaled * gain - gated * factor
        dy_ref[:, sl] = (d_gated * silu).astype(bf16)
        dgate_ref[:, sl] = (d_gated * y * (sig + silu * (1.0 - sig))).astype(bf16)
        ggain_ref[0:1, sl] += jnp.sum(scaled * gated, axis=0, keepdims=True)
    result = dot_nn(mixed_ref[...], wo_ref[...])
    each = pl.num_programs(0) // shares

    @pl.when(pl.program_id(0) < (shares - 1) * each)
    def _():
        sent_ref[...] = result.astype(bf16)

    @pl.when(pl.program_id(0) >= (shares - 1) * each)
    def _():
        kept_ref[...] = result


def gated_specs(shares, normed, y):
    length, model = normed.shape
    channels = y.shape[1]
    blocks = length // SPAN
    each, at = rows_in_order(shares, blocks)

    def rows(size):
        return pl.BlockSpec((SPAN, size), lambda i, s: (at(i, s), 0))

    def whole(shape):
        return pl.BlockSpec(shape, lambda i, s: (0, 0))

    ins = [rows(model), whole((model, channels)), rows(channels), whole((channels, model)), whole((1, channels))]
    parts = [pl.BlockSpec((SPAN, model), lambda i, s: (i % each, 0))] * shares
    return blocks, each, at, rows, whole, ins, parts


def gate_step(shares, where, normed, w_z, y, w_out, gain, cot_parts):
    length, model = normed.shape
    channels = y.shape[1]
    blocks, each, at, rows, whole, ins, parts = gated_specs(shares, normed, y)
    tall = pl.BlockSpec((model // 2, SPAN), lambda i, s: (0, at(i, s)))
    return pl.pallas_call(
        functools.partial(gate_kernel, shares),
        grid_spec=pltpu.PrefetchScalarGridSpec(
            num_scalar_prefetch=1,
            grid=(blocks,),
            in_specs=ins + parts,
            out_specs=[pl.BlockSpec((8, SPAN), lambda i, s: (0, at(i, s))), tall, tall],
            scratch_shapes=[pltpu.VMEM((SPAN, model), bf16)],
        ),
        out_shape=[
            jax.ShapeDtypeStruct((8, length), f32), jax.ShapeDtypeStruct((model // 2, length), bf16),
            jax.ShapeDtypeStruct((model // 2, length), bf16),
        ],
        compiler_params=pltpu.CompilerParams(vmem_limit_bytes=20 * 2**20),
        cost_estimate=pl.CostEstimate(flops=4 * length * model * channels, bytes_accessed=8 * length * channels, transcendentals=0),
    )(where, normed, w_z, y, w_out, gain, *cot_parts)


def norm_step(shares, inner, where, normed, w_z, y, w_out, gain, stats, cot_parts):
    length, model = normed.shape
    channels = y.shape[1]
    blocks, each, at, rows, whole, ins, parts = gated_specs(shares, normed, y)
    many = (shares - 1) * each
    return pl.pallas_call(
        functools.partial(norm_kernel, shares, inner),
        grid_spec=pltpu.PrefetchScalarGridSpec(
            num_scalar_prefetch=1,
            grid=(blocks,),
            in_specs=ins + [pl.BlockSpec((8, SPAN), lambda i, s: (0, at(i, s)))] + parts,
            out_specs=[
                rows(channels), rows(channels), rows(channels), whole((8, channels)),
                pl.BlockSpec((SPAN, model), lambda i, s: (jnp.minimum(i, many - 1), 0)),
                pl.BlockSpec((SPAN, model), lambda i, s: (jnp.maximum(i - many, 0), 0)),
            ],
            scratch_shapes=[
                pltpu.VMEM((SPAN, model), bf16), pltpu.VMEM((SPAN, channels), f32), pltpu.VMEM((SPAN, channels), f32)
            ],
        ),
        out_shape=[jax.ShapeDtypeStruct((length, channels), bf16)] * 3
        + [
            jax.ShapeDtypeStruct((8, channels), f32), jax.ShapeDtypeStruct((many * SPAN, model), bf16),
            jax.ShapeDtypeStruct((each * SPAN, model), f32),
        ],
        compiler_params=pltpu.CompilerParams(vmem_limit_bytes=26 * 2**20),
        cost_estimate=pl.CostEstimate(flops=6 * length * model * channels, bytes_accessed=18 * length * channels, transcendentals=0),
    )(where, normed, w_z, y, w_out, gain, stats, *cot_parts)


def cut_kernel(size, where_ref, source_ref, sent_ref, kept_ref, turned):
    turned[...] = source_ref[...].T
    for i in range(sent_ref.shape[0] // size):
        to = slice(i * size, (i + 1) * size)
        sent_ref[to] = turned[pl.ds(pl.multiple_of((2 * i + 1 - where_ref[2]) * size, size), size)]
        kept_ref[to] = turned[pl.ds(pl.multiple_of((2 * i + where_ref[2]) * size, size), size)]


def cut_step(groups, where, source):
    length, model = source.shape
    out = pl.BlockSpec((model // 2, length), lambda i, s: (0, 0))
    return pl.pallas_call(
        functools.partial(cut_kernel, model // groups),
        grid_spec=pltpu.PrefetchScalarGridSpec(
            num_scalar_prefetch=1,
            grid=(1,),
            in_specs=[pl.BlockSpec((length, model), lambda i, s: (0, 0))],
            out_specs=[out, out],
            scratch_shapes=[pltpu.VMEM((model, length), bf16)],
        ),
        out_shape=[jax.ShapeDtypeStruct((model // 2, length), bf16)] * 2,
        compiler_params=pltpu.CompilerParams(vmem_limit_bytes=14 * 2**20),
        cost_estimate=pl.CostEstimate(flops=0, bytes_accessed=4 * length * model, transcendentals=0),
    )(where, source)


def base_kernel(gate_ref, wz_ref, value_ref, wx_ref, out_ref):
    out_ref[...] = dot_nt(gate_ref[...], wz_ref[...]) + dot_nt(value_ref[...], wx_ref[...])


def base_step(d_gate, w_z, d_value, w_x):
    length, channels = d_gate.shape
    model = w_z.shape[0]
    width = d_value.shape[1]

    def rows(size):
        return pl.BlockSpec((SPAN, size), lambda b: (b, 0))

    return pl.pallas_call(
        base_kernel,
        grid=(length // SPAN,),
        in_specs=[
            rows(channels), pl.BlockSpec((model, channels), lambda b: (0, 0)), rows(width),
            pl.BlockSpec((model, width), lambda b: (0, 0)),
        ],
        out_specs=rows(model),
        out_shape=jax.ShapeDtypeStruct((length, model), f32),
        compiler_params=pltpu.CompilerParams(vmem_limit_bytes=13 * 2**20),
        cost_estimate=pl.CostEstimate(flops=3 * length * channels * model, bytes_accessed=8 * length * channels, transcendentals=0),
    )(d_gate, w_z, d_value, w_x)


def last_kernel(shares, where_ref, *refs):
    own, parts, refs = refs[:shares], refs[shares : 2 * shares], refs[2 * shares :]
    dv_ref, one_ref, two_ref, base_ref, wx_ref, wb_ref, wd_ref, sent_ref, kept_ref, low_ref, gain_ref, u_ref = refs

    @pl.when(pl.program_id(0) == 0)
    def _():
        gain_ref[...] = jnp.zeros_like(gain_ref)

    pick_part(shares, parts, u_ref)
    low = own[0][...]
    for ref in own[1:]:
        low = low + ref[...]
    low = low.astype(bf16)
    low_ref[...] = low
    steps = jnp.concatenate([one_ref[...], two_ref[...]], axis=1).astype(bf16)
    total = dot_nt(dv_ref[...], wx_ref[...]) + dot_nt(low, wb_ref[...]) + dot_nn(steps, wd_ref[...]) + base_ref[...]
    u = u_ref[...].astype(f32)
    scale = lax.rsqrt(jnp.sum(u * u, axis=1, keepdims=True) * (1.0 / u.shape[1]) + 1e-05)
    gain_ref[0:1] += jnp.sum(total * (u * scale), axis=0, keepdims=True)
    each = pl.num_programs(0) // shares

    @pl.when(pl.program_id(0) < (shares - 1) * each)
    def _():
        sent_ref[...] = total.astype(bf16)

    @pl.when(pl.program_id(0) >= (shares - 1) * each)
    def _():
        kept_ref[...] = total


def last_step(shares, where, d_bcs, u_parts, d_value, steps, base, w_x, share_bc, w_dt):
    length, width = d_value.shape
    model = base.shape[1]
    blocks = length // SPAN
    each, at = rows_in_order(shares, blocks)

    def rows(size):
        return pl.BlockSpec((SPAN, size), lambda i, s: (at(i, s), 0))

    def whole(value):
        return pl.BlockSpec(value.shape, lambda i, s: (0, 0))

    many = (shares - 1) * each
    narrow = d_bcs[0].shape[1]
    return pl.pallas_call(
        functools.partial(last_kernel, shares),
        grid_spec=pltpu.PrefetchScalarGridSpec(
            num_scalar_prefetch=1,
            grid=(blocks,),
            in_specs=[rows(narrow)] * shares
            + [pl.BlockSpec((SPAN, model), lambda i, s: (i % each, 0))] * shares
            + [rows(width), rows(steps[0].shape[1]), rows(steps[1].shape[1]), rows(model)]
            + [pl.BlockSpec((model, width), lambda i, s: (0, 1)), whole(share_bc), whole(w_dt)],
            out_specs=[
                pl.BlockSpec((SPAN, model), lambda i, s: (jnp.minimum(i, many - 1), 0)),
                pl.BlockSpec((SPAN, model), lambda i, s: (jnp.maximum(i - many, 0), 0)),
                rows(narrow),
                pl.BlockSpec((8, model), lambda i, s: (0, 0)),
            ],
            scratch_shapes=[pltpu.VMEM((SPAN, model), bf16)],
        ),
        out_shape=[
            jax.ShapeDtypeStruct((many * SPAN, model), bf16), jax.ShapeDtypeStruct((each * SPAN, model), f32),
            jax.ShapeDtypeStruct((length, narrow), bf16), jax.ShapeDtypeStruct((8, model), f32),
        ],
        compiler_params=pltpu.CompilerParams(vmem_limit_bytes=56 * 2**20),
        cost_estimate=pl.CostEstimate(flops=2 * length * width * model, bytes_accessed=8 * length * model, transcendentals=0),
    )(where, *d_bcs, *u_parts, d_value, *steps, base, w_x, share_bc, w_dt)


def input_kernel(tensor, *refs):
    parts, (u_ref, gain_ref, out_ref) = refs[:-3], refs[-3:]
    d_part = parts[0][...]
    for ref in parts[1:]:
        d_part = d_part + ref[...].astype(f32)
    u = u_ref[...].astype(f32)
    model = u.shape[1]
    scale = lax.rsqrt(jnp.sum(u * u, axis=1, keepdims=True) * (1.0 / model) + 1e-05)
    weighted = d_part * gain_ref[...]
    dot = jnp.sum(weighted * u, axis=1, keepdims=True)
    d_input = (scale * weighted - u * (scale * scale * scale * (dot * (1.0 / model)))).astype(bf16)
    width = model // tensor
    for i in range(tensor):
        out_ref[i] = d_input[:, i * width : (i + 1) * width]


def input_step(tensor, parts, u_part, norm_gain):
    rows_in, model = u_part.shape
    rows = pl.BlockSpec((SPAN, model), lambda b: (b, 0))
    return pl.pallas_call(
        functools.partial(input_kernel, tensor),
        grid=(rows_in // SPAN,),
        in_specs=[rows] * (len(parts) + 1) + [pl.BlockSpec((1, model), lambda b: (0, 0))],
        out_specs=pl.BlockSpec((tensor, SPAN, model // tensor), lambda b: (0, b, 0)),
        out_shape=jax.ShapeDtypeStruct((tensor, rows_in, model // tensor), bf16),
        compiler_params=pltpu.CompilerParams(vmem_limit_bytes=10 * 2**20),
        cost_estimate=pl.CostEstimate(flops=10 * rows_in * model, bytes_accessed=10 * rows_in * model, transcendentals=0),
    )(*parts, u_part, norm_gain)


def finish_kernel(tensor, model, wide, heads, cells, where_ref, last_ref, *out_refs):
    width = last_ref.shape[2]
    lines = (last_ref.shape[1] - cells) // 3
    parts = None
    for i in range(tensor):
        for n in (2, 1, 0):
            piece = last_ref[i, cells + n * lines : cells + (n + 1) * lines].astype(f32)
            parts = piece if parts is None else parts + piece
    conv_ref, bias_ref, gain_ref, step_ref, decay_ref, skip_ref, norm_ref, bc_ref, bc_bias_ref = out_refs
    conv_ref[...] = parts[0:4]
    bias_ref[...] = parts[4]
    gain_ref[...] = parts[5]
    for n, ref in enumerate((step_ref, decay_ref, skip_ref)):
        ref[...] = parts[6, n * heads : (n + 1) * heads]

    def shared(start, size):
        return parts[7 + start // width, start % width : start % width + size]

    size = model // tensor
    norm = shared(0, size)
    at = jnp.full((size,), where_ref[3], jnp.int32)
    for i in range(1, tensor):
        norm = jnp.where(at == i, shared(i * size, size), norm)
    norm_ref[...] = norm
    for n in range(4):
        bc_ref[n] = shared(model + n * wide, wide)
    bc_bias_ref[...] = shared(model + 4 * wide, wide)


def finish_step(where, last, cells, model, wide, heads):
    tensor, _, width = last.shape
    shapes = [(4, width), (width,), (width,), (heads,), (heads,), (heads,), (model // tensor,), (4, wide), (wide,)]
    return pl.pallas_call(
        functools.partial(finish_kernel, tensor, model, wide, heads, cells),
        grid_spec=pltpu.PrefetchScalarGridSpec(
            num_scalar_prefetch=1,
            grid=(1,),
            in_specs=[pl.BlockSpec(last.shape, lambda i, s: (0, 0, 0))],
            out_specs=[pl.BlockSpec(v, lambda i, s, rank=len(v): (0,) * rank) for v in shapes],
        ),
        out_shape=[jax.ShapeDtypeStruct(v, f32) for v in shapes],
        compiler_params=pltpu.CompilerParams(vmem_limit_bytes=6 * 2**20),
    )(where, last)


EPS = 1e-05
AXES = ("g", "c", "t")


def tie(value, *others):
    return lax.optimization_barrier((value, *others))[0]


def row_major(value):
    return with_layout_constraint(value, Layout(major_to_minor=tuple(range(value.ndim))))


def thirds(value):
    parts = []
    for _ in range(3):
        part = lax.reduce_precision(value, 8, 7)
        parts.append(part.astype(bf16))
        value = value - part
    return parts


def side_by_side(value, width):
    each = width // value.shape[1]
    rows = value.shape[0] // each
    return jnp.concatenate([value[i * rows : (i + 1) * rows] for i in range(each)], axis=1)


def one_by_one(value, width):
    return jnp.concatenate([value[:, i : i + width] for i in range(0, value.shape[1], width)], axis=0)


def order_by_xor(pieces, index):
    bit = 1
    while bit < len(pieces):
        flip = (index & bit) != 0
        pieces = [jnp.where(flip, pieces[i ^ bit], pieces[i]) for i in range(len(pieces))]
        bit *= 2
    return pieces


class Plan:
    def __init__(self, groups, tensor, per_dp):
        self.groups, self.tensor, self.per_dp = groups, tensor, per_dp
        self.k = tensor // (2 * per_dp)
        self.shares = 2 * self.k
        self.seqs = 2 * per_dp
        self.t = lax.axis_index("t")
        self.c = lax.axis_index("c")
        self.g = lax.axis_index("g")
        self.seq = self.t // self.k
        self.share = self.c * self.k + self.t % self.k
        self.piece = (self.seq % per_dp) * self.shares + self.share
        self.bits = [1 << b for b in range(groups.bit_length() - 1)]

    def send(self, value, where):
        def number(g, c, t):
            return (g * 2 + c) * self.tensor + t

        pairs = [
            (number(g, c, t), number(*where(g, c, t)))
            for g in range(self.groups) for c in range(2) for t in range(self.tensor)
        ]
        return lax.ppermute(value, AXES, pairs)

    def across(self, value, e):
        k = self.k

        def where(g, c, t):
            other = (c * k + t % k) ^ e
            return g, other // k, t // k * k + other % k

        return self.send(value, where)

    def around(self, value, e):
        return self.send(value, lambda g, c, t: (g ^ e, c, t))

    def along(self, value, e):
        return self.send(value, lambda g, c, t: (g, c, t ^ (e * self.k)))

    def swap_for_sequence(self, sources):
        per_dp, length, width = sources[0].shape
        halves = [v.reshape(per_dp, 2, length // 2, width) for v in sources]
        sent = jnp.stack([lax.dynamic_index_in_dim(v, 1 - self.c, 1, keepdims=False) for v in halves])
        got = self.send(sent, lambda g, c, t: (g, 1 - c, t))
        out = []
        for i, v in enumerate(halves):
            kept = lax.dynamic_index_in_dim(v, self.c, 1, keepdims=False)
            out.append(jnp.concatenate(order_by_xor([kept, got[i]], self.c), axis=0))
        return out

    def to_sequence(self, source):
        seqs, rows, width = source.shape
        return lax.all_to_all(source.reshape(self.tensor, rows // self.k, width), "t", 0, 0, tiled=True)

    def pieces_of_sequence(self, got):
        return jnp.concatenate([got[i] for i in range(self.tensor)], axis=1)

    def blocks_back(self, source):
        width = source.shape[1] // self.tensor
        return jnp.stack([source[:, i * width : (i + 1) * width] for i in range(self.tensor)])

    def from_sequence(self, blocks):
        got = lax.all_to_all(blocks, "t", 0, 0, tiled=True)
        return got.reshape(self.seqs, self.k * blocks.shape[1], blocks.shape[2])

    def pieces_of_batch(self, got):
        per_dp = self.per_dp
        kept = lax.dynamic_slice_in_dim(got, self.c * per_dp, per_dp, 0)
        sent = lax.dynamic_slice_in_dim(got, (1 - self.c) * per_dp, per_dp, 0)
        other = self.send(sent, lambda g, c, t: (g, 1 - c, t))
        return jnp.concatenate(order_by_xor([kept, other], self.c), axis=1)

    def gather_shares(self, part):
        got = [part] + [self.across(part, e) for e in range(1, self.shares)]
        return jnp.concatenate(order_by_xor(got, self.share), axis=0)

    def sum_part(self, whole, axis, wire):
        size = whole.shape[axis] // self.shares
        total = lax.dynamic_slice_in_dim(whole, self.share * size, size, axis)
        for e in range(1, self.shares):
            other = lax.dynamic_slice_in_dim(whole, (self.share ^ e) * size, size, axis).astype(wire)
            total = total + self.across(other, e).astype(f32)
        return total

    def sum_shares(self, value):
        e = 1
        while e < self.shares:
            value = value + self.across(value, e)
            e *= 2
        return value

    def slot(self, value, j):
        def where(g, c, t):
            share = t // 2
            return g, share // self.k, (2 * c + (j ^ (t & 1))) * self.k + share % self.k

        return self.send(value, where)

    def unslot(self, value, j1, j0):
        def where(g, c, t):
            seq, share = t // self.k, c * self.k + t % self.k
            return g, j1 ^ (seq >> 1), 2 * share + (j0 ^ (seq & 1))

        return self.send(value, where)

    def slice_of(self, whole):
        size = whole.shape[0] // self.groups
        return lax.dynamic_slice_in_dim(whole, self.g * size, size, 0)

    def spread(self, piece, first, until=None):
        held = piece[None]
        bits = self.bits if first else self.bits[::-1]
        offsets = [0]
        for bit in bits:
            got = self.around(held, bit)
            more = [off | bit for off in offsets]
            if bit == bits[-1]:
                return [held, got if until is None else tie(got, until)], [offsets, more]
            held = jnp.concatenate([held, got], axis=0)
            offsets = offsets + more

    def halves(self, source, first):
        bit = self.bits[0] if first else self.bits[-1]
        size = source.shape[1] // self.groups
        own = self.g & bit
        out = []
        for at in (bit - own, own):
            blocks = [
                lax.dynamic_slice_in_dim(source, (r + at) * size, size, 1) for r in range(self.groups) if not r & bit
            ]
            out.append(jnp.concatenate(blocks, axis=1))
        return out

    def first_send(self, sent, first):
        return self.around(sent, self.bits[0] if first else self.bits[-1])

    def next_sums(self, held, first, after=()):
        bits = self.bits[1:] if first else self.bits[-2::-1]
        left = len(bits)
        held = held.reshape((2,) * left + (-1, held.shape[-1]))
        for bit in bits:
            axis = left - 1 if first else 0
            mine = ((self.g & bit) != 0).astype(jnp.int32)
            sent = lax.dynamic_index_in_dim(held, 1 - mine, axis, keepdims=False).astype(bf16)
            kept = lax.dynamic_index_in_dim(held, mine, axis, keepdims=False)
            got = self.around(sent, bit)
            left -= 1
            if left == 0:
                return sent, kept, got
            held = kept + got.astype(f32)

    def slot_blocks(self, held):
        half = held[0].shape[-2] // 2
        return [
            lax.dynamic_slice_in_dim(value, (j1 ^ (self.seq >> 1)) * half, half, value.ndim - 2).astype(bf16)
            for value in held for j1 in (0, 1)
        ]

    def slot_sends(self, blocks, slots):
        return [self.unslot(blocks[2 * i + j1], j1, j0) for i, j0 in enumerate(slots) for j1 in (0, 1)]

    def slot_total(self, got):
        return sum(v.astype(f32) for v in got)


def per_device(
    groups, tensor,
    inputs, segment, cotangent, norm_gain, weight_z, weight_x, weight_bc, weight_dt, conv_weight_x, conv_bias_x,
    conv_weight_bc, conv_bias_bc, step_bias, decay_log, skip_gain, gate_gain, weight_out,
):
    plan = Plan(groups, tensor, inputs.shape[0])
    shares = plan.shares
    length = inputs.shape[1]
    model = norm_gain.shape[0]
    width = conv_bias_x.shape[0]
    heads = step_bias.shape[0]
    wide = conv_bias_bc.shape[0]
    inner = width * tensor
    two = (0, 1)

    other = plan.send(segment, lambda g, c, t: (g, 1 - c, t))
    both_seg = jnp.where(plan.c == 0, jnp.concatenate([segment, other]), jnp.concatenate([other, segment]))
    seg = lax.dynamic_index_in_dim(both_seg, plan.seq, 0, keepdims=False)
    blocks = seg.reshape(length // SPAN, SPAN)
    ends = blocks[:, -1]
    starts = jnp.concatenate([jnp.full((1,), -1, jnp.int32), ends[:-1]])
    flags = [(blocks == starts[:, None]).reshape(length), (blocks == ends[:, None]).reshape(length)]
    flags += [jnp.concatenate([jnp.zeros((k,), bool), seg[k:] == seg[:-k]]) for k in (1, 2, 3)]
    flags += [jnp.concatenate([seg[k:] == seg[:-k], jnp.zeros((k,), bool)]) for k in (1, 2, 3)]
    aux = jnp.stack(flags, axis=1).astype(f32)
    seg_column, seg_row = seg[:, None], seg[None]
    head_row = jnp.zeros((1, width), f32)
    head_row = lax.dynamic_update_slice(head_row, jnp.concatenate([step_bias, decay_log, skip_gain])[None], (0, 0))
    exact = jnp.concatenate([conv_weight_x, conv_bias_x[None], gate_gain[None], head_row], axis=0)
    row_count = exact.shape[0]
    riders = [weight_dt.T.reshape(-1, width)] + thirds(exact)
    dt_rows = riders[0].shape[0]
    riders = jnp.concatenate(riders, axis=0)
    riders = jnp.pad(riders, ((0, -riders.shape[0] % 16), (0, 0)))
    mine_x = jnp.concatenate([plan.slice_of(weight_x), riders], axis=0)
    size = model // groups
    x_slots = [plan.slot(mine_x, j) for j in two]
    riders = [x_slots[j][size:] for j in two]
    mine_o = plan.slice_of(weight_out)
    mine = jnp.stack([plan.slice_of(weight_z), jnp.concatenate([mine_o[:, i : i + width] for i in range(0, model, width)], axis=0)])
    zo_slots = [plan.slot(tie(mine, *x_slots), j) for j in two]
    swapped_u, swapped_cot = plan.swap_for_sequence([inputs, cotangent])
    spread_x = [plan.spread(x_slots[j][:size], j == 0) for j in two]
    got_u = plan.to_sequence(tie(swapped_u, aux, seg_column, seg_row, spread_x[0][0][0], spread_x[1][0][0], *zo_slots))
    stacks, moves = [], []
    for j in two:
        found, offsets = spread_x[j]
        for stack, offs in zip(found, offsets):
            moves += [
                (len(stacks), (i,), slice(0, size), 0, size, off, slice(j * width, (j + 1) * width))
                for i, off in enumerate(offs)
            ]
            stacks.append(stack)
    w_x = assemble(moves, plan.g, stacks, (model, 2 * width))
    all_z = plan.spread(jnp.stack([zo_slots[j][0] for j in two]), True)
    all_o = plan.spread(jnp.stack([zo_slots[j][1] for j in two]), False)
    share_bc = lax.dynamic_slice_in_dim(weight_bc, plan.share * (wide // shares), wide // shares, 1)
    w_dt = [v[:dt_rows].reshape(heads, model) for v in riders]
    slots = [
        sum(v[dt_rows + i * row_count : dt_rows + (i + 1) * row_count].astype(f32) for i in (2, 1, 0)) for v in riders
    ]
    rows = jnp.concatenate(slots, axis=1)
    conv_w, conv_b, gain = rows[0:4], rows[4:5], rows[5:6]
    bias, log_rate, skip = (
        jnp.concatenate([v[6:7, i * heads : (i + 1) * heads] for v in slots], axis=1) for i in range(3)
    )
    w_dt = jnp.concatenate(w_dt, axis=0)
    rate, skip_lanes = -jnp.exp(log_rate), jnp.repeat(skip, HEAD, axis=1)
    where = jnp.stack([plan.share, (plan.g & plan.bits[-1]) // plan.bits[-1], plan.g & 1, plan.t])
    got_u = tie(
        got_u, w_x, all_z[0][0], all_o[0][0], share_bc, w_dt, conv_w, conv_b, gain, bias, rate, skip_lanes, where, swapped_cot
    )
    got_cot = plan.to_sequence(tie(swapped_cot, got_u))
    u_part_low = plan.pieces_of_sequence(got_u)
    u_part = u_part_low.astype(f32)
    scale_part = lax.rsqrt(jnp.mean(u_part * u_part, axis=-1, keepdims=True) + EPS)
    normed = lax.optimization_barrier(plan.gather_shares((u_part * scale_part * norm_gain).astype(bf16)))

    bc_pre = dot_nn(normed, weight_bc)
    common = (
        dot_nn(normed, w_x), bc_pre, dot_nt(normed, w_dt) + bias, rate, aux, seg_column, seg_row,
        conv_w, conv_b, conv_weight_bc, conv_bias_bc[None], skip_lanes,
    )
    y, entering, steps, cum_t = forward_scan(common)

    z_stacks, o_stacks = tie((all_z[0], all_o[0]), y)
    moves = [
        (n, (i, j), slice(0, size), 0, size, off, slice(j * width, (j + 1) * width))
        for n in two for i, off in enumerate(all_z[1][n]) for j in two
    ]
    w_z = assemble(moves, plan.g, z_stacks, (model, 2 * width))
    tall = width // groups
    moves = [
        (n, (i, j), slice(m * tall, (m + 1) * tall), j * width, tall, off, slice(m * width, (m + 1) * width))
        for n in two for i, off in enumerate(all_o[1][n]) for j in two for m in range(model // width)
    ]
    w_out = assemble(moves, plan.g, o_stacks, (2 * width, model))
    cot_part = plan.pieces_of_sequence(tie(got_cot, y))
    cot_parts = [cot_part] + [plan.across(cot_part, e) for e in range(1, shares)]
    stats, c_sent, c_kept = gate_step(shares, where, normed, w_z, y, w_out, gain, cot_parts)
    mixed, d_y, d_gate, grad_gain, sent_y, out_part = norm_step(
        shares, inner, where, normed, w_z, y, w_out, gain, plan.sum_shares(stats), cot_parts
    )
    rows_per = length // shares
    for e in range(1, shares):
        out_part = out_part + plan.across(sent_y[(shares - 1 - e) * rows_per : (shares - e) * rows_per], e).astype(f32)
    out_low = (u_part_low.astype(f32) + out_part).astype(bf16)
    out_blocks = plan.blocks_back(out_low)
    got_out = plan.from_sequence(out_blocks)
    grad_gain = grad_gain[0]

    x_sent, x_kept = cut_step(groups, where, normed)
    sent_z = dot_nn(x_sent, d_gate).astype(bf16)
    sent_o = dot_nn(c_sent, mixed).astype(bf16)
    early_z = plan.first_send(sent_z, True)
    early_o = plan.first_send(sent_o, False)

    def slots_of(value):
        return [value[:, j * width : (j + 1) * width] for j in two]

    back = [backward_scan(common, 0, shares, where, steps, cum_t, y, tie(d_y, sent_z, sent_o, out_blocks), entering)]
    early_z, early_o = tie((early_z, early_o), back[0][1])
    next_z, held_z, late_z = plan.next_sums(dot_nn(x_kept, d_gate) + early_z.astype(f32), True)
    next_o, held_o, late_o = plan.next_sums(dot_nn(c_kept, mixed) + early_o.astype(f32), False)
    first = tie(back[0][1], next_z, next_o, got_out)
    sent_x = dot_nn(x_sent, first).astype(bf16)
    early_x = plan.first_send(sent_x, True)
    kept_x = dot_nn(x_kept, first)
    base = base_step(d_gate, w_z, first, w_x)
    late_z, late_o = tie((late_z, late_o), sent_x, kept_x, base)
    late_z = held_z + late_z.astype(f32)
    late_o = held_o + late_o.astype(f32)
    zo_blocks = plan.slot_blocks([jnp.stack(v) for v in zip(slots_of(late_z), slots_of(late_o))])
    back.append(backward_scan(common, 1, shares, where, steps, cum_t, y, tie(d_y, zo_blocks), entering, back[0][0]))
    zo_sums = plan.slot_sends(zo_blocks, two)
    u_parts = [u_part_low] + [plan.across(tie(u_part_low, y), e) for e in range(1, shares)]
    back[1] = tie(back[1], zo_sums, early_x)

    next_x, held_x, late_x = plan.next_sums(kept_x + tie(early_x, back[1][1]).astype(f32), True)
    d_bcs = [back[1][0][0]] + [plan.across(back[1][0][e], e) for e in range(1, shares)]
    sent_d, d_part, low_bc, grad_norm = last_step(
        shares, where, d_bcs, u_parts, back[1][1], (back[0][2], back[1][2]), tie(base, next_x, held_x), w_x, share_bc, w_dt
    )
    x0_blocks = plan.slot_blocks([held_x + tie(late_x, sent_d).astype(f32)])
    x0_sums = plan.slot_sends(x0_blocks, (0,))
    grad_norm = grad_norm[0]
    d_parts = [d_part] + [
        plan.across(sent_d[(shares - 1 - e) * rows_per : (shares - e) * rows_per], e) for e in range(1, shares)
    ]
    back_blocks = input_step(tensor, d_parts, tie(u_part_low, x0_blocks), norm_gain[None])
    got_back = plan.from_sequence(back_blocks)
    output = plan.pieces_of_batch(tie(got_out, back_blocks))

    rows = []
    for j in two:
        g_conv, g_heads = back[j][3], back[j][5]
        head_row = jnp.zeros((1, width), f32)
        g_skip = jnp.sum(g_conv[5].reshape(-1, HEAD), axis=1)
        head_row = lax.dynamic_update_slice(head_row, jnp.concatenate([g_heads[0], g_heads[1], g_skip])[None], (0, 0))
        rows.append(jnp.concatenate([g_conv[0:5], grad_gain[None, j * width : (j + 1) * width], head_row], axis=0))
    order = [rows[0], rows[1]]
    flip = (plan.seq & 1) != 0
    order = [jnp.where(flip, rows[1 - j], rows[j]) for j in two]
    shared = jnp.concatenate([grad_norm, (back[0][4] + back[1][4])[0:5].reshape(-1)])
    shared = jnp.pad(shared, (0, -shared.shape[0] % width)).reshape(-1, width)
    small = jnp.concatenate(order + [shared], axis=0)
    count = rows[0].shape[0]

    rest = jnp.concatenate([low_bc, back[0][2].astype(bf16), back[1][2].astype(bf16)], axis=1)
    size_r = model // groups
    sent_r, kept_r = (
        one_by_one(lax.dot_general(u, v, (((0,), (1,)), ((), ())), preferred_element_type=f32), size_r)
        for u, v in ((rest, x_sent), (tie(rest, back_blocks), x_kept))
    )
    pack = None
    for n, bit in enumerate(plan.bits):
        beside = side_by_side(sent_r.astype(bf16), width)
        message = jnp.concatenate([beside] + thirds(small), axis=0)
        pack = message if pack is None else pack
        got = plan.around(message, bit)
        if n == 0:
            got = tie(got, back_blocks)
        tall, lines = beside.shape[0], small.shape[0]
        kept_r = kept_r + one_by_one(got[:tall], size_r).astype(f32)
        small = small + sum(got[tall + i * lines : tall + (i + 1) * lines].astype(f32) for i in (2, 1, 0))
        if n + 1 < len(plan.bits):
            parts = groups >> (n + 1)
            held = kept_r.reshape(parts // 2, 2, kept_r.shape[0] // parts, size_r)
            mine = ((plan.g & plan.bits[n + 1]) != 0).astype(jnp.int32)
            sent_r, kept_r = (
                lax.dynamic_index_in_dim(held, v, 1, keepdims=False).reshape(-1, size_r) for v in (1 - mine, mine)
            )
    rest = kept_r

    final = tie(back[1][1], pack)
    early_r = plan.first_send(dot_nn(x_sent, final).astype(bf16), True)
    kept_x1 = lax.optimization_barrier(dot_nn(x_kept, tie(final, back_blocks)))
    next_r, held_r, late_r = plan.next_sums(kept_x1 + tie(early_r, back_blocks).astype(f32), True)
    late_r = held_r + late_r.astype(f32)
    grad_z, grad_out = plan.slot_total(zo_sums)
    grad_out = grad_out.T
    input_grad = cotangent.astype(f32) + plan.pieces_of_batch(got_back).astype(f32)

    beyond = wide // shares
    parts = [rest[:beyond]] + [
        jnp.where(flip, rest[beyond + (1 - j) * heads : beyond + (2 - j) * heads], rest[beyond + j * heads : beyond + (j + 1) * heads])
        for j in two
    ]
    rest = jnp.concatenate(parts, axis=0).astype(bf16)
    half = size_r // 2
    columns = rest.shape[0]
    rests, smalls = [], []
    for e in range(shares):
        rows_e = lax.dynamic_slice_in_dim(rest, ((plan.share ^ e) // plan.k) * half, half, 1)
        rests.append(plan.across(rows_e, e) if e else rows_e)
        smalls.append(plan.across(small, e) if e else small)
    rests = side_by_side(jnp.concatenate(order_by_xor(rests, plan.share), axis=0), width)
    smalls = order_by_xor(smalls, plan.share)
    shared = sum(v[2 * count :] for v in smalls)
    smalls = jnp.stack([
        jnp.concatenate([smalls[i // 2][(i % 2) * count : (i % 2 + 1) * count], shared], axis=0) for i in range(tensor)
    ])
    cells = rests.shape[0]
    rests = jnp.broadcast_to(rests[None], (tensor, cells, width))
    last = jnp.concatenate([rests] + thirds(smalls), axis=1)
    last = tie(last, next_r)
    x1_sums = plan.slot_sends(plan.slot_blocks([tie(late_r, last)]), (1,))
    last = lax.all_to_all(tie(last, got_back), "t", 0, 0, tiled=True).reshape(tensor, -1, width)
    grad_x = plan.slot_total(tie(x0_sums + x1_sums, last))
    rests = one_by_one(jnp.sum(last[:, :cells].astype(f32), axis=0), half)
    rests = [rests[i * columns : (i + 1) * columns] for i in range(shares)]
    grad_bc = jnp.concatenate([v[:beyond] for v in rests], axis=0).T
    dts = [v[beyond + j * heads : beyond + (j + 1) * heads] for v in rests for j in two]
    grad_dt = lax.dynamic_index_in_dim(jnp.stack(dts), plan.t, 0, keepdims=False).T
    g_conv, g_conv_bias, g_gain, g_step, g_decay, g_skip, g_norm, g_conv_bc, g_conv_bc_bias = finish_step(
        where, last, cells, model, wide, heads
    )
    return (
        output, input_grad, g_norm, grad_z, grad_x, grad_bc, grad_dt, g_conv, g_conv_bias, g_conv_bc, g_conv_bc_bias,
        g_step, g_decay, g_skip, g_gain, grad_out,
    )


def solution(mesh):
    data, tensor = mesh.shape["dp"], mesh.shape["tensor"]
    groups = data // 2
    fine = Mesh(mesh.devices.reshape(groups, 2, tensor), AXES)
    dp = ("g", "c")

    def step(*args):
        return per_device(groups, tensor, *args)

    return jax.shard_map(
        step,
        mesh=fine,
        in_specs=(
            P(dp, None, "t"), P(dp, None), P(dp, None, "t"), P(), P(None, "t"), P(None, "t"), P(), P(None, "t"),
            P(None, "t"), P("t"), P(), P(), P("t"), P("t"), P("t"), P("t"), P("t", None),
        ),
        out_specs=(
            P(dp, None, "t"), P(dp, None, "t"), P("t"), P(dp, "t"), P(dp, "t"), P(dp, None), P(dp, "t"),
            P(None, "t"), P("t"), P(), P(), P("t"), P("t"), P("t"), P("t"), P("t", dp),
        ),
        check_vma=False,
    )
```

```python
import functools

import jax
import jax.numpy as jnp
from jax import lax
from jax.experimental import pallas as pl
from jax.experimental.layout import Layout, with_layout_constraint
from jax.experimental.pallas import tpu as pltpu
from jax.sharding import Mesh
from jax.sharding import PartitionSpec as P

SPAN = 256
HEAD = 64
LANES = 128
LOG2E = 1.4426950408889634
FAR = -1e30
bf16 = jnp.bfloat16
f32 = jnp.float32


def dot_nn(a, b):
    return lax.dot_general(a, b, (((1,), (0,)), ((), ())), preferred_element_type=f32)


def dot_nt(a, b):
    return lax.dot_general(a, b, (((1,), (1,)), ((), ())), preferred_element_type=f32)


def dot_tn(a, b):
    return lax.dot_general(a, b, (((0,), (0,)), ((), ())), preferred_element_type=f32)


def split_dot(a, b, flip=False):
    one = a.astype(bf16)
    two = (a - one.astype(f32)).astype(bf16)
    if flip:
        return dot_nn(b, one) + dot_nn(b, two)
    return dot_nn(one, b) + dot_nn(two, b)


def conv_terms(scr, block, halo, masks):
    span = block.shape[0]
    scr[0:8, :] = halo
    scr[8 : 8 + span, :] = block
    return [block] + [scr[8 - k : 8 - k + span, :] * masks(1 + k) for k in (1, 2, 3)]


def conv_sum(terms, weights, bias):
    total = bias + weights[3:4] * terms[0]
    for k in (1, 2, 3):
        total = total + weights[3 - k : 4 - k] * terms[k]
    return total


def sigmoid(v):
    return 0.5 + 0.5 * jnp.tanh(0.5 * v)


def lanes_of(columns, pair, low):
    return jnp.where(low, columns[:, 2 * pair : 2 * pair + 1], columns[:, 2 * pair + 1 : 2 * pair + 2])


def steps_of(pre, rate, lower, upper):
    dt = jnp.maximum(pre, 0.0) + jnp.log1p(jnp.exp(-jnp.abs(pre)))
    decay = dt * (rate * LOG2E)
    cum, cum_t = None, None
    for _ in range(3):
        part = decay.astype(bf16)
        decay = decay - part.astype(f32)
        one, two = dot_nn(lower, part), dot_tn(part, upper)
        cum, cum_t = (one, two) if cum is None else (cum + one, cum_t + two)
    return dt, cum, cum_t


def forward_kernel(
    v_ref, vh_ref, bc_ref, bch_ref, pre_ref, rate_ref, aux_ref, segc_ref, segr_ref,
    cw_ref, cb_ref, cwb_ref, cbb_ref, skip_ref,
    y_ref, hprev_ref, steps_ref, cumt_ref, state, scr, scrb, far_ref, mask_ref,
):
    span = v_ref.shape[0]
    pairs = v_ref.shape[1] // LANES
    n = bc_ref.shape[1] // 2

    @pl.when(pl.program_id(0) == 0)
    def _():
        state[...] = jnp.zeros_like(state)

    aux = aux_ref[...]
    for i in range(5):
        mask_ref[i] = jnp.broadcast_to(aux[:, i : i + 1], (span, LANES))
    bc_act = conv_sum(conv_terms(scrb, bc_ref[...], bch_ref[...], lambda i: aux[:, i : i + 1]), cwb_ref[...], cbb_ref[...])
    bc_act = bc_act * sigmoid(bc_act)
    b_mat = bc_act[:, :n].astype(bf16)
    c_mat = bc_act[:, n:].astype(bf16)
    scores = dot_nt(c_mat, b_mat)
    later = lax.broadcasted_iota(jnp.int32, (span, span), 0)
    earlier = lax.broadcasted_iota(jnp.int32, (span, span), 1)
    lower = (later >= earlier).astype(f32).astype(bf16)
    upper = (earlier >= later).astype(f32).astype(bf16)
    dt, cum, cum_t = steps_of(pre_ref[...], rate_ref[...], lower, upper)
    far_ref[...] = jnp.where((segc_ref[...] == segr_ref[...]) & (later >= earlier), 0.0, FAR)
    low = lax.broadcasted_iota(jnp.int32, (1, LANES), 1) < HEAD
    steps_ref[...] = jnp.concatenate([dt, cum, sigmoid(pre_ref[...])], axis=1)
    cumt_ref[...] = cum_t
    half = span // 2
    for p in range(pairs):
        sl = slice(p * LANES, (p + 1) * LANES)
        act = conv_sum(conv_terms(scr, v_ref[:, sl], vh_ref[:, sl], lambda i: mask_ref[i]), cw_ref[:, sl], cb_ref[:, sl])
        x = act * sigmoid(act)
        v = (x * lanes_of(dt, p, low)).astype(bf16)
        inside = None
        for e in (0, 1):
            h = 2 * p + e
            mine = jnp.where(low if e == 0 else ~low, v, jnp.zeros_like(v))
            part = []
            for rows, columns in ((slice(0, half), slice(0, half)), (slice(half, span), slice(0, span))):
                spread = (cum[rows, h : h + 1] - cum_t[h : h + 1, columns]) + far_ref[rows, columns]
                mixing = (scores[rows, columns] * jnp.exp2(spread)).astype(bf16)
                part.append(dot_nn(mixing, mine[columns]))
            part = jnp.concatenate(part, axis=0)
            inside = part if inside is None else inside + part
        wide_cum = lanes_of(cum, p, low)
        enter = jnp.exp2(wide_cum) * mask_ref[0]
        tail = jnp.exp2(wide_cum[span - 1 : span] - wide_cum) * mask_ref[1]
        prior = state[:, sl]
        low_prior = prior.astype(bf16)
        hprev_ref[0, :, sl] = low_prior
        outside = dot_nn(c_mat, low_prior) * enter
        y_ref[:, sl] = inside + outside + skip_ref[:, sl] * x
        weighted = (tail * v.astype(f32)).astype(bf16)
        state[:, sl] = enter[span - 1 : span] * prior + dot_tn(b_mat, weighted)


def backward_kernel(
    first, more, shares, where_ref,
    v_ref, vh_ref, bc_ref, bch_ref, steps_ref, rate_ref, aux_ref, segc_ref, segr_ref,
    cw_ref, cb_ref, cwb_ref, cbb_ref, skip_ref, cumt_ref, y_ref, dy_ref, hprev_ref, *rest,
):
    if more:
        before_refs, rest = rest[:shares], rest[shares:]
    dbc_refs, rest = rest[:shares], rest[shares:]
    (
        dv_ref, ddelta_ref, gx_ref, gbc_ref, gh_ref,
        dstate, after, afterb, scr, scrb, far_ref, dscore, dot_y, dot_x, last, tailed, entered, mask_ref,
    ) = rest
    span = v_ref.shape[0]
    channels = v_ref.shape[1]
    pairs = channels // LANES
    heads = channels // HEAD
    everyone = steps_ref.shape[1] // 3
    dt, cum, slope_dt = (steps_ref[:, i * everyone + first : i * everyone + first + heads] for i in range(3))
    rate = rate_ref[:, first : first + heads]
    half = span // 2
    n = bc_ref.shape[1] // 2

    @pl.when(pl.program_id(0) == 0)
    def _():
        for ref in (dstate, after, afterb, gx_ref, gbc_ref, gh_ref):
            ref[...] = jnp.zeros_like(ref)

    aux = aux_ref[...]
    for i in range(8):
        mask_ref[i] = jnp.broadcast_to(aux[:, i : i + 1], (span, LANES))
    terms_bc = conv_terms(scrb, bc_ref[...], bch_ref[...], lambda i: aux[:, i : i + 1])
    act_bc = conv_sum(terms_bc, cwb_ref[...], cbb_ref[...])
    sig_bc = sigmoid(act_bc)
    bc_act = act_bc * sig_bc
    b_mat = bc_act[:, :n].astype(bf16)
    c_mat = bc_act[:, n:].astype(bf16)
    scores = dot_nt(b_mat, c_mat)
    earlier = lax.broadcasted_iota(jnp.int32, (span, span), 0)
    later = lax.broadcasted_iota(jnp.int32, (span, span), 1)
    far_ref[...] = jnp.where((segc_ref[...] == segr_ref[...]) & (later >= earlier), 0.0, FAR)
    low = lax.broadcasted_iota(jnp.int32, (1, LANES), 1) < HEAD
    upper = (later >= earlier).astype(f32).astype(bf16)
    dscore[...] = jnp.zeros_like(dscore)

    def rows_of(value):
        return jnp.sum(value, axis=0, keepdims=True)

    for p in range(pairs):
        sl = slice(p * LANES, (p + 1) * LANES)
        terms = conv_terms(scr, v_ref[:, sl], vh_ref[:, sl], lambda i: mask_ref[i])
        act = conv_sum(terms, cw_ref[:, sl], cb_ref[:, sl])
        sig = sigmoid(act)
        x = act * sig
        dt_lanes = lanes_of(dt, p, low)
        v = (x * dt_lanes).astype(bf16)
        v_wide = v.astype(f32)
        dy = dy_ref[:, sl]
        dy_wide = dy.astype(f32)
        d_inside = None
        for e in (0, 1):
            h = 2 * p + e
            mask = low if e == 0 else ~low
            mine = jnp.where(mask, dy, jnp.zeros_like(dy))
            part = []
            for rows, columns in ((slice(0, half), slice(0, span)), (slice(half, span), slice(half, span))):
                spread = (cumt_ref[first + h : first + h + 1, columns] - cum[rows, h : h + 1]) + far_ref[rows, columns]
                kernel = jnp.exp2(spread)
                mixing = (scores[rows, columns] * kernel).astype(bf16)
                part.append(dot_nn(mixing, mine[columns]))
                dscore[rows, columns] += dot_nt(v[rows], mine[columns]) * kernel
            part = jnp.concatenate(part, axis=0)
            d_inside = part if d_inside is None else d_inside + part
        wide_cum = lanes_of(cum, p, low)
        enter = jnp.exp2(wide_cum) * mask_ref[0]
        tail = jnp.exp2(wide_cum[span - 1 : span] - wide_cum) * mask_ref[1]
        d_new = dstate[:, sl]
        low_new = d_new.astype(bf16)
        d_outer = dot_nn(b_mat, low_new) * tail
        dval = d_inside + d_outer
        skip = skip_ref[:, sl]
        dot_y[:, sl] = dy_wide * (y_ref[:, sl] - skip * x) - v_wide * dval
        dot_x[:, sl] = x * dval
        entering = (enter * dy_wide).astype(bf16)
        entered[:, sl] = entering
        tailed[:, sl] = (tail * v_wide).astype(bf16)
        prior = hprev_ref[0, :, sl]
        carried = enter[span - 1 : span]
        last[:, sl] = rows_of(v_wide * d_outer) + carried * rows_of(prior.astype(f32) * d_new)
        dx = dt_lanes * dval + skip * dy_wide
        dconv = dx * (sig * (1.0 + act * (1.0 - sig)))
        scr[0:span, :] = dconv
        scr[span : span + 8, :] = after[:, sl]
        d_pre = cw_ref[3:4, sl] * dconv
        for k in (1, 2, 3):
            d_pre = d_pre + cw_ref[3 - k : 4 - k, sl] * (scr[k : k + span, :] * mask_ref[4 + k])
        dv_ref[:, sl] = d_pre.astype(bf16)
        after[:, sl] = dconv[0:8]
        for k in (0, 1, 2, 3):
            gx_ref[3 - k : 4 - k, sl] += rows_of(dconv * terms[k])
        gx_ref[4:5, sl] += rows_of(dconv)
        gx_ref[5:6, sl] += rows_of(dy_wide * x)

    ds = dscore[...].astype(bf16)
    d_b = dot_nn(ds, c_mat) + dot_nt(tailed[...], dstate[...].astype(bf16))
    d_c = dot_tn(ds, b_mat) + dot_nt(entered[...], hprev_ref[0])
    slope = sig_bc * (1.0 + act_bc * (1.0 - sig_bc))
    dconv_bc = jnp.concatenate([d_b, d_c], axis=1) * slope
    scrb[0:span, :] = dconv_bc
    scrb[span : span + 8, :] = afterb[...]
    d_pre = cwb_ref[3:4] * dconv_bc
    for k in (1, 2, 3):
        d_pre = d_pre + cwb_ref[3 - k : 4 - k] * (scrb[k : k + span, :] * aux[:, 4 + k : 5 + k])
    cut = 2 * n // shares
    pieces = [d_pre[:, s * cut : (s + 1) * cut] for s in range(shares)]
    own = jnp.full((span, cut), where_ref[0], jnp.int32)
    bit = 1
    while bit < shares:
        pieces = [jnp.where((own & bit) != 0, pieces[s ^ bit], pieces[s]) for s in range(shares)]
        bit *= 2
    for e in range(shares):
        dbc_refs[e][...] = pieces[e] + before_refs[e][...] if more else pieces[e]
    afterb[...] = dconv_bc[0:8]
    for k in (0, 1, 2, 3):
        gbc_ref[3 - k : 4 - k] += rows_of(dconv_bc * terms_bc[k])
    gbc_ref[4:5] += rows_of(dconv_bc)

    for p in range(pairs):
        sl = slice(p * LANES, (p + 1) * LANES)
        carried = jnp.exp2(lanes_of(cum[span - 1 : span], p, low)) * aux[span - 1 : span, 0:1]
        dstate[:, sl] = carried * dstate[:, sl] + dot_tn(c_mat, entered[:, sl])

    place = lax.broadcasted_iota(jnp.int32, (channels, heads), 0) // HEAD
    head = lax.broadcasted_iota(jnp.int32, (channels, heads), 1)
    select = (place == head).astype(bf16)
    d_cum = split_dot(dot_y[...], select)
    final = split_dot(jnp.broadcast_to(last[...], (8, channels)), select)[0:1]
    row = lax.broadcasted_iota(jnp.int32, (span, heads), 0)
    d_cum = d_cum + jnp.where(row == span - 1, final, 0.0)
    d_decay = split_dot(d_cum, upper, flip=True)
    d_dt = split_dot(dot_x[...], select) + d_decay * rate
    d_delta = d_dt * slope_dt
    ddelta_ref[...] = d_delta.astype(bf16)
    gh_ref[0:1] += rows_of(d_delta)
    gh_ref[1:2] += rows_of(d_decay * dt * rate)


def scan_specs(common, width, column, reverse):
    length, channels = common[0].shape
    wide, heads = common[1].shape[1], common[2].shape[1]
    blocks = length // SPAN
    tall = SPAN // 8

    def at(b):
        return blocks - 1 - b if reverse else b

    def rows(size, at_column=0):
        return pl.BlockSpec((SPAN, size), lambda b, *_: (at(b), at_column))

    def halo(size, at_column=0):
        return pl.BlockSpec((8, size), lambda b, *_: (jnp.maximum(at(b) * tall - 1, 0), at_column))

    def whole(shape, at_column=0):
        return pl.BlockSpec(shape, lambda b, *_: (0, at_column))

    states = pl.BlockSpec((1, wide // 2, width), lambda b, *_: (at(b), 0, column))
    ins = [
        rows(width, column), halo(width, column), rows(wide), halo(wide), rows(heads), whole((1, heads)), rows(8), rows(1),
        pl.BlockSpec((1, SPAN), lambda b, *_: (0, at(b))),
        whole((4, width), column), whole((1, width), column), whole((4, wide)), whole((1, wide)),
        whole((1, width), column),
    ]
    return blocks, rows, whole, states, ins


def forward_scan(common):
    v_pre, bc_pre, pre = common[:3]
    length, channels = v_pre.shape
    wide, heads = bc_pre.shape[1], pre.shape[1]
    blocks, rows, whole, states, ins = scan_specs(common, channels, 0, False)
    return pl.pallas_call(
        forward_kernel,
        grid=(blocks,),
        in_specs=ins,
        out_specs=[rows(channels), states, rows(3 * heads), pl.BlockSpec((heads, SPAN), lambda b: (0, b))],
        out_shape=[
            jax.ShapeDtypeStruct((length, channels), f32),
            jax.ShapeDtypeStruct((blocks, wide // 2, channels), bf16),
            jax.ShapeDtypeStruct((length, 3 * heads), f32), jax.ShapeDtypeStruct((heads, length), f32),
        ],
        scratch_shapes=[
            pltpu.VMEM((wide // 2, channels), f32), pltpu.VMEM((SPAN + 8, LANES), f32),
            pltpu.VMEM((SPAN + 8, wide), f32), pltpu.VMEM((SPAN, SPAN), f32), pltpu.VMEM((5, SPAN, LANES), f32),
        ],
        compiler_params=pltpu.CompilerParams(vmem_limit_bytes=20 * 2**20),
        cost_estimate=pl.CostEstimate(flops=channels * length, bytes_accessed=channels * length, transcendentals=0),
    )(v_pre, v_pre, bc_pre, bc_pre, *common[2:])


def backward_scan(common, half, shares, where, steps, cum_t, y, dy, hprev, before=()):
    v_pre, bc_pre, pre = common[:3]
    length, channels = v_pre.shape[0], v_pre.shape[1] // 2
    wide, heads = bc_pre.shape[1], pre.shape[1] // 2
    blocks, rows, whole, states, ins = scan_specs(common, channels, half, True)
    split = rows(wide // shares)
    ins[4] = rows(steps.shape[1])
    sums = pl.BlockSpec((2 * heads, SPAN), lambda b, *_: (0, blocks - 1 - b))
    out = pl.pallas_call(
        functools.partial(backward_kernel, half * heads, bool(before), shares),
        grid_spec=pltpu.PrefetchScalarGridSpec(
            num_scalar_prefetch=1,
            grid=(blocks,),
            in_specs=ins + [sums, rows(channels, half), rows(channels, half), states] + [split] * len(before),
            out_specs=[split] * shares
            + [rows(channels), rows(heads), whole((8, channels)), whole((8, wide)), whole((8, heads))],
            scratch_shapes=[
                pltpu.VMEM((wide // 2, channels), f32), pltpu.VMEM((8, channels), f32), pltpu.VMEM((8, wide), f32),
                pltpu.VMEM((SPAN + 8, LANES), f32), pltpu.VMEM((SPAN + 8, wide), f32), pltpu.VMEM((SPAN, SPAN), f32),
                pltpu.VMEM((SPAN, SPAN), f32), pltpu.VMEM((SPAN, channels), f32), pltpu.VMEM((SPAN, channels), f32),
                pltpu.VMEM((1, channels), f32), pltpu.VMEM((SPAN, channels), bf16), pltpu.VMEM((SPAN, channels), bf16),
                pltpu.VMEM((8, SPAN, LANES), f32),
            ],
        ),
        out_shape=[jax.ShapeDtypeStruct((length, wide // shares), f32)] * shares
        + [
            jax.ShapeDtypeStruct((length, channels), bf16), jax.ShapeDtypeStruct((length, heads), bf16),
            jax.ShapeDtypeStruct((8, channels), f32), jax.ShapeDtypeStruct((8, wide), f32),
            jax.ShapeDtypeStruct((8, heads), f32),
        ],
        compiler_params=pltpu.CompilerParams(vmem_limit_bytes=56 * 2**20),
        cost_estimate=pl.CostEstimate(flops=channels * length, bytes_accessed=channels * length, transcendentals=0),
    )(where, v_pre, v_pre, bc_pre, bc_pre, steps, *common[3:], cum_t, y, dy, hprev, *before)
    return tuple(out[:shares]), *out[shares:]


def assemble(moves, index, sources, shape):
    def kernel(index_ref, *refs):
        out_ref = refs[-1]
        at = index_ref[0]
        for source, lead, rows, base, stride, offset, columns in moves:
            start = pl.multiple_of(base + (at ^ offset) * stride, stride)
            out_ref[pl.ds(start, rows.stop - rows.start), columns] = refs[source][(*lead, rows, slice(None))]

    return pl.pallas_call(
        kernel,
        grid_spec=pltpu.PrefetchScalarGridSpec(
            num_scalar_prefetch=1,
            grid=(1,),
            in_specs=[pl.BlockSpec(v.shape, lambda i, s, rank=v.ndim: (0,) * rank) for v in sources],
            out_specs=pl.BlockSpec(shape, lambda i, s: (0, 0)),
        ),
        out_shape=jax.ShapeDtypeStruct(shape, bf16),
        compiler_params=pltpu.CompilerParams(vmem_limit_bytes=10 * 2**20),
        cost_estimate=pl.CostEstimate(flops=0, bytes_accessed=4 * shape[0] * shape[1], transcendentals=0),
    )(index.reshape(1), *sources)


def rows_in_order(shares, blocks):
    each = blocks // shares

    def at(i, where_ref):
        return (where_ref[0] ^ (shares - 1 - i // each)) * each + i % each

    return each, at


def pick_part(shares, parts, cot):
    each = pl.num_programs(0) // shares
    for e in range(shares):
        @pl.when(pl.program_id(0) // each == shares - 1 - e)
        def _(e=e):
            cot[...] = parts[e][...]


def gate_kernel(shares, where_ref, normed_ref, wz_ref, y_ref, wo_ref, gain_ref, *refs):
    parts, (stats_ref, sent_ref, kept_ref, cot) = refs[:shares], refs[shares:]
    span, model = cot.shape
    pick_part(shares, parts, cot)
    half = model // 2
    sent_ref[...] = cot[:, pl.ds(pl.multiple_of((1 - where_ref[1]) * half, half), half)].T
    kept_ref[...] = cot[:, pl.ds(pl.multiple_of(where_ref[1] * half, half), half)].T
    gate = dot_nn(normed_ref[...], wz_ref[...])
    d_mixed = dot_nt(cot[...], wo_ref[...])
    gated = y_ref[...] * (gate * sigmoid(gate))
    squares = jnp.sum(gated * gated, axis=1, keepdims=True)
    product = jnp.sum(d_mixed * gain_ref[...] * gated, axis=1, keepdims=True)
    lane = lax.broadcasted_iota(jnp.int32, (span, LANES), 1)
    both = jnp.where(lane == 0, squares, jnp.where(lane == 1, product, 0.0))
    stats_ref[...] = both.T[0:8]


def norm_kernel(
    shares, inner, where_ref, normed_ref, wz_ref, y_ref, wo_ref, gain_ref, stats_ref, *refs
):
    parts, refs = refs[:shares], refs[shares:]
    mixed_ref, dy_ref, dgate_ref, ggain_ref, sent_ref, kept_ref, cot, gate_ref, dmix_ref = refs

    @pl.when(pl.program_id(0) == 0)
    def _():
        ggain_ref[...] = jnp.zeros_like(ggain_ref)

    pick_part(shares, parts, cot)
    gate_ref[...] = dot_nn(normed_ref[...], wz_ref[...])
    dmix_ref[...] = dot_nt(cot[...], wo_ref[...])
    stats = jnp.concatenate([stats_ref[...]] + [jnp.zeros((LANES - 8, stats_ref.shape[1]), f32)], axis=0).T
    scale = lax.rsqrt(stats[:, 0:1] * (1.0 / inner) + 1e-05)
    factor = scale * scale * scale * (stats[:, 1:2] * (1.0 / inner))
    for at in range(0, y_ref.shape[1], LANES):
        sl = slice(at, at + LANES)
        y, gate, gain = y_ref[:, sl], gate_ref[:, sl], gain_ref[:, sl]
        sig = sigmoid(gate)
        silu = gate * sig
        gated = y * silu
        scaled = dmix_ref[:, sl] * scale
        mixed_ref[:, sl] = (gated * scale * gain).astype(bf16)
        d_gated = scaled * gain - gated * factor
        dy_ref[:, sl] = (d_gated * silu).astype(bf16)
        dgate_ref[:, sl] = (d_gated * y * (sig + silu * (1.0 - sig))).astype(bf16)
        ggain_ref[0:1, sl] += jnp.sum(scaled * gated, axis=0, keepdims=True)
    result = dot_nn(mixed_ref[...], wo_ref[...])
    each = pl.num_programs(0) // shares

    @pl.when(pl.program_id(0) < (shares - 1) * each)
    def _():
        sent_ref[...] = result.astype(bf16)

    @pl.when(pl.program_id(0) >= (shares - 1) * each)
    def _():
        kept_ref[...] = result.astype(bf16)


def gated_specs(shares, normed, y):
    length, model = normed.shape
    channels = y.shape[1]
    blocks = length // SPAN
    each, at = rows_in_order(shares, blocks)

    def rows(size):
        return pl.BlockSpec((SPAN, size), lambda i, s: (at(i, s), 0))

    def whole(shape):
        return pl.BlockSpec(shape, lambda i, s: (0, 0))

    ins = [rows(model), whole((model, channels)), rows(channels), whole((channels, model)), whole((1, channels))]
    parts = [pl.BlockSpec((SPAN, model), lambda i, s: (i % each, 0))] * shares
    return blocks, each, at, rows, whole, ins, parts


def gate_step(shares, where, normed, w_z, y, w_out, gain, cot_parts):
    length, model = normed.shape
    channels = y.shape[1]
    blocks, each, at, rows, whole, ins, parts = gated_specs(shares, normed, y)
    tall = pl.BlockSpec((model // 2, SPAN), lambda i, s: (0, at(i, s)))
    return pl.pallas_call(
        functools.partial(gate_kernel, shares),
        grid_spec=pltpu.PrefetchScalarGridSpec(
            num_scalar_prefetch=1,
            grid=(blocks,),
            in_specs=ins + parts,
            out_specs=[pl.BlockSpec((8, SPAN), lambda i, s: (0, at(i, s))), tall, tall],
            scratch_shapes=[pltpu.VMEM((SPAN, model), bf16)],
        ),
        out_shape=[
            jax.ShapeDtypeStruct((8, length), f32), jax.ShapeDtypeStruct((model // 2, length), bf16),
            jax.ShapeDtypeStruct((model // 2, length), bf16),
        ],
        compiler_params=pltpu.CompilerParams(vmem_limit_bytes=20 * 2**20),
        cost_estimate=pl.CostEstimate(flops=4 * length * model * channels, bytes_accessed=8 * length * channels, transcendentals=0),
    )(where, normed, w_z, y, w_out, gain, *cot_parts)


def norm_step(shares, inner, where, normed, w_z, y, w_out, gain, stats, cot_parts):
    length, model = normed.shape
    channels = y.shape[1]
    blocks, each, at, rows, whole, ins, parts = gated_specs(shares, normed, y)
    many = (shares - 1) * each
    return pl.pallas_call(
        functools.partial(norm_kernel, shares, inner),
        grid_spec=pltpu.PrefetchScalarGridSpec(
            num_scalar_prefetch=1,
            grid=(blocks,),
            in_specs=ins + [pl.BlockSpec((8, SPAN), lambda i, s: (0, at(i, s)))] + parts,
            out_specs=[
                rows(channels), rows(channels), rows(channels), whole((8, channels)),
                pl.BlockSpec((SPAN, model), lambda i, s: (jnp.minimum(i, many - 1), 0)),
                pl.BlockSpec((SPAN, model), lambda i, s: (jnp.maximum(i - many, 0), 0)),
            ],
            scratch_shapes=[
                pltpu.VMEM((SPAN, model), bf16), pltpu.VMEM((SPAN, channels), f32), pltpu.VMEM((SPAN, channels), f32)
            ],
        ),
        out_shape=[jax.ShapeDtypeStruct((length, channels), bf16)] * 3
        + [
            jax.ShapeDtypeStruct((8, channels), f32), jax.ShapeDtypeStruct((many * SPAN, model), bf16),
            jax.ShapeDtypeStruct((each * SPAN, model), bf16),
        ],
        compiler_params=pltpu.CompilerParams(vmem_limit_bytes=26 * 2**20),
        cost_estimate=pl.CostEstimate(flops=6 * length * model * channels, bytes_accessed=18 * length * channels, transcendentals=0),
    )(where, normed, w_z, y, w_out, gain, stats, *cot_parts)


def cut_kernel(size, where_ref, source_ref, sent_ref, kept_ref, turned):
    turned[...] = source_ref[...].T
    for i in range(sent_ref.shape[0] // size):
        to = slice(i * size, (i + 1) * size)
        sent_ref[to] = turned[pl.ds(pl.multiple_of((2 * i + 1 - where_ref[2]) * size, size), size)]
        kept_ref[to] = turned[pl.ds(pl.multiple_of((2 * i + where_ref[2]) * size, size), size)]


def cut_step(groups, where, source):
    length, model = source.shape
    out = pl.BlockSpec((model // 2, length), lambda i, s: (0, 0))
    return pl.pallas_call(
        functools.partial(cut_kernel, model // groups),
        grid_spec=pltpu.PrefetchScalarGridSpec(
            num_scalar_prefetch=1,
            grid=(1,),
            in_specs=[pl.BlockSpec((length, model), lambda i, s: (0, 0))],
            out_specs=[out, out],
            scratch_shapes=[pltpu.VMEM((model, length), bf16)],
        ),
        out_shape=[jax.ShapeDtypeStruct((model // 2, length), bf16)] * 2,
        compiler_params=pltpu.CompilerParams(vmem_limit_bytes=14 * 2**20),
        cost_estimate=pl.CostEstimate(flops=0, bytes_accessed=4 * length * model, transcendentals=0),
    )(where, source)


def base_kernel(gate_ref, wz_ref, value_ref, wx_ref, out_ref):
    out_ref[...] = (dot_nt(gate_ref[...], wz_ref[...]) + dot_nt(value_ref[...], wx_ref[...])).astype(bf16)


def base_step(d_gate, w_z, d_value, w_x):
    length, channels = d_gate.shape
    model = w_z.shape[0]
    width = d_value.shape[1]

    def rows(size):
        return pl.BlockSpec((SPAN, size), lambda b: (b, 0))

    return pl.pallas_call(
        base_kernel,
        grid=(length // SPAN,),
        in_specs=[
            rows(channels), pl.BlockSpec((model, channels), lambda b: (0, 0)), rows(width),
            pl.BlockSpec((model, width), lambda b: (0, 0)),
        ],
        out_specs=rows(model),
        out_shape=jax.ShapeDtypeStruct((length, model), bf16),
        compiler_params=pltpu.CompilerParams(vmem_limit_bytes=56 * 2**20),
        cost_estimate=pl.CostEstimate(flops=3 * length * channels * model, bytes_accessed=8 * length * channels, transcendentals=0),
    )(d_gate, w_z, d_value, w_x)


def last_kernel(shares, where_ref, *refs):
    own, parts, refs = refs[:shares], refs[shares : 2 * shares], refs[2 * shares :]
    dv_ref, one_ref, two_ref, base_ref, wx_ref, wb_ref, wd_ref, sent_ref, kept_ref, low_ref, gain_ref, u_ref = refs

    @pl.when(pl.program_id(0) == 0)
    def _():
        gain_ref[...] = jnp.zeros_like(gain_ref)

    pick_part(shares, parts, u_ref)
    low = own[0][...]
    for ref in own[1:]:
        low = low + ref[...]
    low = low.astype(bf16)
    low_ref[...] = low
    steps = jnp.concatenate([one_ref[...].astype(f32), two_ref[...].astype(f32)], axis=1).astype(bf16)
    total = dot_nt(dv_ref[...], wx_ref[...]) + dot_nt(low, wb_ref[...]) + dot_nn(steps, wd_ref[...])
    total = total + base_ref[...].astype(f32)
    u = u_ref[...].astype(f32)
    scale = lax.rsqrt(jnp.sum(u * u, axis=1, keepdims=True) * (1.0 / u.shape[1]) + 1e-05)
    gain_ref[0:1] += jnp.sum(total * (u * scale), axis=0, keepdims=True)
    each = pl.num_programs(0) // shares

    @pl.when(pl.program_id(0) < (shares - 1) * each)
    def _():
        sent_ref[...] = total.astype(bf16)

    @pl.when(pl.program_id(0) >= (shares - 1) * each)
    def _():
        kept_ref[...] = total.astype(bf16)


def last_step(shares, where, d_bcs, u_parts, d_value, steps, base, w_x, share_bc, w_dt):
    length, width = d_value.shape
    model = base.shape[1]
    blocks = length // SPAN
    each, at = rows_in_order(shares, blocks)

    def rows(size):
        return pl.BlockSpec((SPAN, size), lambda i, s: (at(i, s), 0))

    def whole(value):
        return pl.BlockSpec(value.shape, lambda i, s: (0, 0))

    many = (shares - 1) * each
    narrow = d_bcs[0].shape[1]
    return pl.pallas_call(
        functools.partial(last_kernel, shares),
        grid_spec=pltpu.PrefetchScalarGridSpec(
            num_scalar_prefetch=1,
            grid=(blocks,),
            in_specs=[rows(narrow)] * shares
            + [pl.BlockSpec((SPAN, model), lambda i, s: (i % each, 0))] * shares
            + [rows(width), rows(steps[0].shape[1]), rows(steps[1].shape[1]), rows(model)]
            + [pl.BlockSpec((model, width), lambda i, s: (0, 1)), whole(share_bc), whole(w_dt)],
            out_specs=[
                pl.BlockSpec((SPAN, model), lambda i, s: (jnp.minimum(i, many - 1), 0)),
                pl.BlockSpec((SPAN, model), lambda i, s: (jnp.maximum(i - many, 0), 0)),
                rows(narrow),
                pl.BlockSpec((8, model), lambda i, s: (0, 0)),
            ],
            scratch_shapes=[pltpu.VMEM((SPAN, model), bf16)],
        ),
        out_shape=[
            jax.ShapeDtypeStruct((many * SPAN, model), bf16), jax.ShapeDtypeStruct((each * SPAN, model), bf16),
            jax.ShapeDtypeStruct((length, narrow), bf16), jax.ShapeDtypeStruct((8, model), f32),
        ],
        compiler_params=pltpu.CompilerParams(vmem_limit_bytes=56 * 2**20),
        cost_estimate=pl.CostEstimate(flops=2 * length * width * model, bytes_accessed=8 * length * model, transcendentals=0),
    )(where, *d_bcs, *u_parts, d_value, *steps, base, w_x, share_bc, w_dt)


def input_kernel(tensor, *refs):
    parts, (u_ref, gain_ref, out_ref) = refs[:-3], refs[-3:]
    d_part = parts[0][...].astype(f32)
    for ref in parts[1:]:
        d_part = d_part + ref[...].astype(f32)
    u = u_ref[...].astype(f32)
    model = u.shape[1]
    scale = lax.rsqrt(jnp.sum(u * u, axis=1, keepdims=True) * (1.0 / model) + 1e-05)
    weighted = d_part * gain_ref[...]
    dot = jnp.sum(weighted * u, axis=1, keepdims=True)
    d_input = (scale * weighted - u * (scale * scale * scale * (dot * (1.0 / model)))).astype(bf16)
    width = model // tensor
    for i in range(tensor):
        out_ref[i] = d_input[:, i * width : (i + 1) * width]


def input_step(tensor, parts, u_part, norm_gain):
    rows_in, model = u_part.shape
    rows = pl.BlockSpec((SPAN, model), lambda b: (b, 0))
    return pl.pallas_call(
        functools.partial(input_kernel, tensor),
        grid=(rows_in // SPAN,),
        in_specs=[rows] * (len(parts) + 1) + [pl.BlockSpec((1, model), lambda b: (0, 0))],
        out_specs=pl.BlockSpec((tensor, SPAN, model // tensor), lambda b: (0, b, 0)),
        out_shape=jax.ShapeDtypeStruct((tensor, rows_in, model // tensor), bf16),
        compiler_params=pltpu.CompilerParams(vmem_limit_bytes=10 * 2**20),
        cost_estimate=pl.CostEstimate(flops=10 * rows_in * model, bytes_accessed=10 * rows_in * model, transcendentals=0),
    )(*parts, u_part, norm_gain)


def finish_kernel(tensor, model, wide, heads, cells, where_ref, last_ref, *out_refs):
    width = last_ref.shape[2]
    lines = (last_ref.shape[1] - cells) // 3
    parts = None
    for i in range(tensor):
        for n in (2, 1, 0):
            piece = last_ref[i, cells + n * lines : cells + (n + 1) * lines].astype(f32)
            parts = piece if parts is None else parts + piece
    conv_ref, bias_ref, gain_ref, step_ref, decay_ref, skip_ref, norm_ref, bc_ref, bc_bias_ref = out_refs
    conv_ref[...] = parts[0:4]
    bias_ref[...] = parts[4]
    gain_ref[...] = parts[5]
    for n, ref in enumerate((step_ref, decay_ref, skip_ref)):
        ref[...] = parts[6, n * heads : (n + 1) * heads]

    def shared(start, size):
        return parts[7 + start // width, start % width : start % width + size]

    size = model // tensor
    norm = shared(0, size)
    at = jnp.full((size,), where_ref[3], jnp.int32)
    for i in range(1, tensor):
        norm = jnp.where(at == i, shared(i * size, size), norm)
    norm_ref[...] = norm
    for n in range(4):
        bc_ref[n] = shared(model + n * wide, wide)
    bc_bias_ref[...] = shared(model + 4 * wide, wide)


def finish_step(where, last, cells, model, wide, heads):
    tensor, _, width = last.shape
    shapes = [(4, width), (width,), (width,), (heads,), (heads,), (heads,), (model // tensor,), (4, wide), (wide,)]
    return pl.pallas_call(
        functools.partial(finish_kernel, tensor, model, wide, heads, cells),
        grid_spec=pltpu.PrefetchScalarGridSpec(
            num_scalar_prefetch=1,
            grid=(1,),
            in_specs=[pl.BlockSpec(last.shape, lambda i, s: (0, 0, 0))],
            out_specs=[pl.BlockSpec(v, lambda i, s, rank=len(v): (0,) * rank) for v in shapes],
        ),
        out_shape=[jax.ShapeDtypeStruct(v, f32) for v in shapes],
        compiler_params=pltpu.CompilerParams(vmem_limit_bytes=6 * 2**20),
    )(where, last)


EPS = 1e-05
AXES = ("g", "c", "t")


def tie(value, *others):
    return lax.optimization_barrier((value, *others))[0]


def row_major(value):
    return with_layout_constraint(value, Layout(major_to_minor=tuple(range(value.ndim))))


def thirds(value):
    parts = []
    for _ in range(3):
        part = lax.reduce_precision(value, 8, 7)
        parts.append(part.astype(bf16))
        value = value - part
    return parts


def side_by_side(value, width):
    each = width // value.shape[1]
    rows = value.shape[0] // each
    return jnp.concatenate([value[i * rows : (i + 1) * rows] for i in range(each)], axis=1)


def one_by_one(value, width):
    return jnp.concatenate([value[:, i : i + width] for i in range(0, value.shape[1], width)], axis=0)


def order_by_xor(pieces, index):
    bit = 1
    while bit < len(pieces):
        flip = (index & bit) != 0
        pieces = [jnp.where(flip, pieces[i ^ bit], pieces[i]) for i in range(len(pieces))]
        bit *= 2
    return pieces


class Plan:
    def __init__(self, groups, tensor, per_dp):
        self.groups, self.tensor, self.per_dp = groups, tensor, per_dp
        self.k = tensor // (2 * per_dp)
        self.shares = 2 * self.k
        self.seqs = 2 * per_dp
        self.t = lax.axis_index("t")
        self.c = lax.axis_index("c")
        self.g = lax.axis_index("g")
        self.seq = self.t // self.k
        self.share = self.c * self.k + self.t % self.k
        self.piece = (self.seq % per_dp) * self.shares + self.share
        self.bits = [1 << b for b in range(groups.bit_length() - 1)]

    def send(self, value, where):
        def number(g, c, t):
            return (g * 2 + c) * self.tensor + t

        pairs = [
            (number(g, c, t), number(*where(g, c, t)))
            for g in range(self.groups) for c in range(2) for t in range(self.tensor)
        ]
        return lax.ppermute(value, AXES, pairs)

    def across(self, value, e):
        k = self.k

        def where(g, c, t):
            other = (c * k + t % k) ^ e
            return g, other // k, t // k * k + other % k

        return self.send(value, where)

    def around(self, value, e):
        return self.send(value, lambda g, c, t: (g ^ e, c, t))

    def along(self, value, e):
        return self.send(value, lambda g, c, t: (g, c, t ^ (e * self.k)))

    def swap_for_sequence(self, sources):
        per_dp, length, width = sources[0].shape
        halves = [v.reshape(per_dp, 2, length // 2, width) for v in sources]
        sent = jnp.stack([lax.dynamic_index_in_dim(v, 1 - self.c, 1, keepdims=False) for v in halves])
        got = self.send(sent, lambda g, c, t: (g, 1 - c, t))
        out = []
        for i, v in enumerate(halves):
            kept = lax.dynamic_index_in_dim(v, self.c, 1, keepdims=False)
            out.append(jnp.concatenate(order_by_xor([kept, got[i]], self.c), axis=0))
        return out

    def to_sequence(self, source):
        seqs, rows, width = source.shape
        return lax.all_to_all(source.reshape(self.tensor, rows // self.k, width), "t", 0, 0, tiled=True)

    def pieces_of_sequence(self, got):
        return jnp.concatenate([got[i] for i in range(self.tensor)], axis=1)

    def blocks_back(self, source):
        width = source.shape[1] // self.tensor
        return jnp.stack([source[:, i * width : (i + 1) * width] for i in range(self.tensor)])

    def from_sequence(self, blocks):
        got = lax.all_to_all(blocks, "t", 0, 0, tiled=True)
        return got.reshape(self.seqs, self.k * blocks.shape[1], blocks.shape[2])

    def pieces_of_batch(self, got):
        per_dp = self.per_dp
        kept = lax.dynamic_slice_in_dim(got, self.c * per_dp, per_dp, 0)
        sent = lax.dynamic_slice_in_dim(got, (1 - self.c) * per_dp, per_dp, 0)
        other = self.send(sent, lambda g, c, t: (g, 1 - c, t))
        return jnp.concatenate(order_by_xor([kept, other], self.c), axis=1)

    def gather_shares(self, part):
        got = [part] + [self.across(part, e) for e in range(1, self.shares)]
        return jnp.concatenate(order_by_xor(got, self.share), axis=0)

    def sum_part(self, whole, axis, wire):
        size = whole.shape[axis] // self.shares
        total = lax.dynamic_slice_in_dim(whole, self.share * size, size, axis)
        for e in range(1, self.shares):
            other = lax.dynamic_slice_in_dim(whole, (self.share ^ e) * size, size, axis).astype(wire)
            total = total + self.across(other, e).astype(f32)
        return total

    def sum_shares(self, value):
        e = 1
        while e < self.shares:
            value = value + self.across(value, e)
            e *= 2
        return value

    def slot(self, value, j):
        def where(g, c, t):
            share = t // 2
            return g, share // self.k, (2 * c + (j ^ (t & 1))) * self.k + share % self.k

        return self.send(value, where)

    def unslot(self, value, j1, j0):
        def where(g, c, t):
            seq, share = t // self.k, c * self.k + t % self.k
            return g, j1 ^ (seq >> 1), 2 * share + (j0 ^ (seq & 1))

        return self.send(value, where)

    def slice_of(self, whole):
        size = whole.shape[0] // self.groups
        return lax.dynamic_slice_in_dim(whole, self.g * size, size, 0)

    def spread(self, piece, first, until=None):
        held = piece[None]
        bits = self.bits if first else self.bits[::-1]
        offsets = [0]
        for bit in bits:
            got = self.around(held, bit)
            more = [off | bit for off in offsets]
            if bit == bits[-1]:
                return [held, got if until is None else tie(got, until)], [offsets, more]
            held = jnp.concatenate([held, got], axis=0)
            offsets = offsets + more

    def halves(self, source, first):
        bit = self.bits[0] if first else self.bits[-1]
        size = source.shape[1] // self.groups
        own = self.g & bit
        out = []
        for at in (bit - own, own):
            blocks = [
                lax.dynamic_slice_in_dim(source, (r + at) * size, size, 1) for r in range(self.groups) if not r & bit
            ]
            out.append(jnp.concatenate(blocks, axis=1))
        return out

    def first_send(self, sent, first):
        return self.around(sent, self.bits[0] if first else self.bits[-1])

    def next_sums(self, held, first, after=()):
        bits = self.bits[1:] if first else self.bits[-2::-1]
        left = len(bits)
        held = held.reshape((2,) * left + (-1, held.shape[-1]))
        for bit in bits:
            axis = left - 1 if first else 0
            mine = ((self.g & bit) != 0).astype(jnp.int32)
            sent = lax.dynamic_index_in_dim(held, 1 - mine, axis, keepdims=False).astype(bf16)
            kept = lax.dynamic_index_in_dim(held, mine, axis, keepdims=False)
            got = self.around(sent, bit)
            left -= 1
            if left == 0:
                return sent, kept, got
            held = kept + got.astype(f32)

    def slot_blocks(self, held):
        half = held[0].shape[-2] // 2
        return [
            lax.dynamic_slice_in_dim(value, (j1 ^ (self.seq >> 1)) * half, half, value.ndim - 2).astype(bf16)
            for value in held for j1 in (0, 1)
        ]

    def slot_sends(self, blocks, slots):
        return [self.unslot(blocks[2 * i + j1], j1, j0) for i, j0 in enumerate(slots) for j1 in (0, 1)]

    def slot_total(self, got):
        return sum(v.astype(f32) for v in got)


def per_device(
    groups, tensor,
    inputs, segment, cotangent, norm_gain, weight_z, weight_x, weight_bc, weight_dt, conv_weight_x, conv_bias_x,
    conv_weight_bc, conv_bias_bc, step_bias, decay_log, skip_gain, gate_gain, weight_out,
):
    plan = Plan(groups, tensor, inputs.shape[0])
    shares = plan.shares
    length = inputs.shape[1]
    model = norm_gain.shape[0]
    width = conv_bias_x.shape[0]
    heads = step_bias.shape[0]
    wide = conv_bias_bc.shape[0]
    inner = width * tensor
    two = (0, 1)

    other = plan.send(segment, lambda g, c, t: (g, 1 - c, t))
    both_seg = jnp.where(plan.c == 0, jnp.concatenate([segment, other]), jnp.concatenate([other, segment]))
    seg = lax.dynamic_index_in_dim(both_seg, plan.seq, 0, keepdims=False)
    blocks = seg.reshape(length // SPAN, SPAN)
    ends = blocks[:, -1]
    starts = jnp.concatenate([jnp.full((1,), -1, jnp.int32), ends[:-1]])
    flags = [(blocks == starts[:, None]).reshape(length), (blocks == ends[:, None]).reshape(length)]
    flags += [jnp.concatenate([jnp.zeros((k,), bool), seg[k:] == seg[:-k]]) for k in (1, 2, 3)]
    flags += [jnp.concatenate([seg[k:] == seg[:-k], jnp.zeros((k,), bool)]) for k in (1, 2, 3)]
    aux = jnp.stack(flags, axis=1).astype(f32)
    seg_column, seg_row = seg[:, None], seg[None]
    head_row = jnp.zeros((1, width), f32)
    head_row = lax.dynamic_update_slice(head_row, jnp.concatenate([step_bias, decay_log, skip_gain])[None], (0, 0))
    exact = jnp.concatenate([conv_weight_x, conv_bias_x[None], gate_gain[None], head_row], axis=0)
    row_count = exact.shape[0]
    riders = [weight_dt.T.reshape(-1, width)] + thirds(exact)
    dt_rows = riders[0].shape[0]
    riders = jnp.concatenate(riders, axis=0)
    riders = jnp.pad(riders, ((0, -riders.shape[0] % 16), (0, 0)))
    mine_x = jnp.concatenate([plan.slice_of(weight_x), riders], axis=0)
    size = model // groups
    x_slots = [plan.slot(mine_x, j) for j in two]
    riders = [x_slots[j][size:] for j in two]
    mine_o = plan.slice_of(weight_out)
    mine = jnp.stack([plan.slice_of(weight_z), jnp.concatenate([mine_o[:, i : i + width] for i in range(0, model, width)], axis=0)])
    zo_slots = [plan.slot(tie(mine, *x_slots), j) for j in two]
    swapped_u, swapped_cot = plan.swap_for_sequence([inputs, cotangent])
    spread_x = [plan.spread(x_slots[j][:size], j == 0) for j in two]
    got_u = plan.to_sequence(tie(swapped_u, aux, seg_column, seg_row, spread_x[0][0][0], spread_x[1][0][0], *zo_slots))
    stacks, moves = [], []
    for j in two:
        found, offsets = spread_x[j]
        for stack, offs in zip(found, offsets):
            moves += [
                (len(stacks), (i,), slice(0, size), 0, size, off, slice(j * width, (j + 1) * width))
                for i, off in enumerate(offs)
            ]
            stacks.append(stack)
    w_x = assemble(moves, plan.g, stacks, (model, 2 * width))
    all_z = plan.spread(jnp.stack([zo_slots[j][0] for j in two]), True)
    all_o = plan.spread(jnp.stack([zo_slots[j][1] for j in two]), False)
    share_bc = lax.dynamic_slice_in_dim(weight_bc, plan.share * (wide // shares), wide // shares, 1)
    w_dt = [v[:dt_rows].reshape(heads, model) for v in riders]
    slots = [
        sum(v[dt_rows + i * row_count : dt_rows + (i + 1) * row_count].astype(f32) for i in (2, 1, 0)) for v in riders
    ]
    rows = jnp.concatenate(slots, axis=1)
    conv_w, conv_b, gain = rows[0:4], rows[4:5], rows[5:6]
    bias, log_rate, skip = (
        jnp.concatenate([v[6:7, i * heads : (i + 1) * heads] for v in slots], axis=1) for i in range(3)
    )
    w_dt = jnp.concatenate(w_dt, axis=0)
    rate, skip_lanes = -jnp.exp(log_rate), jnp.repeat(skip, HEAD, axis=1)
    where = jnp.stack([plan.share, (plan.g & plan.bits[-1]) // plan.bits[-1], plan.g & 1, plan.t])
    got_u = tie(
        got_u, w_x, all_z[0][0], all_o[0][0], share_bc, w_dt, conv_w, conv_b, gain, bias, rate, skip_lanes, where, swapped_cot
    )
    got_cot = plan.to_sequence(tie(swapped_cot, got_u))
    u_part_low = plan.pieces_of_sequence(got_u)
    u_part = u_part_low.astype(f32)
    scale_part = lax.rsqrt(jnp.mean(u_part * u_part, axis=-1, keepdims=True) + EPS)
    normed = lax.optimization_barrier(plan.gather_shares((u_part * scale_part * norm_gain).astype(bf16)))

    bc_pre = dot_nn(normed, weight_bc)
    common = (
        dot_nn(normed, w_x), bc_pre, dot_nt(normed, w_dt) + bias, rate, aux, seg_column, seg_row,
        conv_w, conv_b, conv_weight_bc, conv_bias_bc[None], skip_lanes,
    )
    y, entering, steps, cum_t = forward_scan(common)

    z_stacks, o_stacks = tie((all_z[0], all_o[0]), y)
    moves = [
        (n, (i, j), slice(0, size), 0, size, off, slice(j * width, (j + 1) * width))
        for n in two for i, off in enumerate(all_z[1][n]) for j in two
    ]
    w_z = assemble(moves, plan.g, z_stacks, (model, 2 * width))
    tall = width // groups
    moves = [
        (n, (i, j), slice(m * tall, (m + 1) * tall), j * width, tall, off, slice(m * width, (m + 1) * width))
        for n in two for i, off in enumerate(all_o[1][n]) for j in two for m in range(model // width)
    ]
    w_out = assemble(moves, plan.g, o_stacks, (2 * width, model))
    cot_part = plan.pieces_of_sequence(tie(got_cot, y))
    cot_parts = [cot_part] + [plan.across(cot_part, e) for e in range(1, shares)]
    stats, c_sent, c_kept = gate_step(shares, where, normed, w_z, y, w_out, gain, cot_parts)
    mixed, d_y, d_gate, grad_gain, sent_y, out_part = norm_step(
        shares, inner, where, normed, w_z, y, w_out, gain, plan.sum_shares(stats), cot_parts
    )
    rows_per = length // shares
    for e in range(1, shares):
        out_part = out_part.astype(f32) + plan.across(sent_y[(shares - 1 - e) * rows_per : (shares - e) * rows_per], e).astype(f32)
    out_low = (u_part_low.astype(f32) + out_part).astype(bf16)
    out_blocks = plan.blocks_back(out_low)
    got_out = plan.from_sequence(out_blocks)
    grad_gain = grad_gain[0]

    x_sent, x_kept = cut_step(groups, where, normed)
    sent_z = dot_nn(x_sent, d_gate).astype(bf16)
    sent_o = dot_nn(c_sent, mixed).astype(bf16)
    early_z = plan.first_send(sent_z, True)
    early_o = plan.first_send(sent_o, False)

    def slots_of(value):
        return [value[:, j * width : (j + 1) * width] for j in two]

    back = [backward_scan(common, 0, shares, where, steps, cum_t, y, tie(d_y, sent_z, sent_o, out_blocks), entering)]
    early_z, early_o = tie((early_z, early_o), back[0][1])
    next_z, held_z, late_z = plan.next_sums(dot_nn(x_kept, d_gate) + early_z.astype(f32), True)
    next_o, held_o, late_o = plan.next_sums(dot_nn(c_kept, mixed) + early_o.astype(f32), False)
    first = tie(back[0][1], next_z, next_o, got_out)
    sent_x = dot_nn(x_sent, first).astype(bf16)
    early_x = plan.first_send(sent_x, True)
    kept_x = dot_nn(x_kept, first)
    base = base_step(d_gate, w_z, first, w_x)
    late_z, late_o = tie((late_z, late_o), sent_x, kept_x, base)
    late_z = held_z + late_z.astype(f32)
    late_o = held_o + late_o.astype(f32)
    zo_blocks = plan.slot_blocks([jnp.stack(v) for v in zip(slots_of(late_z), slots_of(late_o))])
    back.append(backward_scan(common, 1, shares, where, steps, cum_t, y, tie(d_y, zo_blocks), entering, back[0][0]))
    zo_sums = plan.slot_sends(zo_blocks, two)
    u_parts = [u_part_low] + [plan.across(tie(u_part_low, y), e) for e in range(1, shares)]
    back[1] = tie(back[1], zo_sums, early_x)

    next_x, held_x, late_x = plan.next_sums(kept_x + tie(early_x, back[1][1]).astype(f32), True)
    d_bcs = [back[1][0][0]] + [plan.across(back[1][0][e], e) for e in range(1, shares)]
    sent_d, d_part, low_bc, grad_norm = last_step(
        shares, where, d_bcs, u_parts, back[1][1], (back[0][2], back[1][2]), tie(base, next_x, held_x), w_x, share_bc, w_dt
    )
    x0_blocks = plan.slot_blocks([held_x + tie(late_x, sent_d).astype(f32)])
    x0_sums = plan.slot_sends(x0_blocks, (0,))
    grad_norm = grad_norm[0]
    d_parts = [d_part] + [
        plan.across(sent_d[(shares - 1 - e) * rows_per : (shares - e) * rows_per], e) for e in range(1, shares)
    ]
    back_blocks = input_step(tensor, d_parts, tie(u_part_low, x0_blocks), norm_gain[None])
    got_back = plan.from_sequence(back_blocks)
    output = plan.pieces_of_batch(tie(got_out, back_blocks))

    rows = []
    for j in two:
        g_conv, g_heads = back[j][3], back[j][5]
        head_row = jnp.zeros((1, width), f32)
        g_skip = jnp.sum(g_conv[5].reshape(-1, HEAD), axis=1)
        head_row = lax.dynamic_update_slice(head_row, jnp.concatenate([g_heads[0], g_heads[1], g_skip])[None], (0, 0))
        rows.append(jnp.concatenate([g_conv[0:5], grad_gain[None, j * width : (j + 1) * width], head_row], axis=0))
    order = [rows[0], rows[1]]
    flip = (plan.seq & 1) != 0
    order = [jnp.where(flip, rows[1 - j], rows[j]) for j in two]
    shared = jnp.concatenate([grad_norm, (back[0][4] + back[1][4])[0:5].reshape(-1)])
    shared = jnp.pad(shared, (0, -shared.shape[0] % width)).reshape(-1, width)
    small = jnp.concatenate(order + [shared], axis=0)
    count = rows[0].shape[0]

    rest = jnp.concatenate([low_bc, back[0][2], back[1][2]], axis=1)
    size_r = model // groups
    sent_r, kept_r = (
        one_by_one(lax.dot_general(u, v, (((0,), (1,)), ((), ())), preferred_element_type=f32), size_r)
        for u, v in ((rest, x_sent), (tie(rest, back_blocks), x_kept))
    )
    pack = None
    for n, bit in enumerate(plan.bits):
        beside = side_by_side(sent_r.astype(bf16), width)
        message = jnp.concatenate([beside] + thirds(small), axis=0)
        pack = message if pack is None else pack
        got = plan.around(message, bit)
        if n == 0:
            got = tie(got, back_blocks)
        tall, lines = beside.shape[0], small.shape[0]
        kept_r = kept_r + one_by_one(got[:tall], size_r).astype(f32)
        small = small + sum(got[tall + i * lines : tall + (i + 1) * lines].astype(f32) for i in (2, 1, 0))
        if n + 1 < len(plan.bits):
            parts = groups >> (n + 1)
            held = kept_r.reshape(parts // 2, 2, kept_r.shape[0] // parts, size_r)
            mine = ((plan.g & plan.bits[n + 1]) != 0).astype(jnp.int32)
            sent_r, kept_r = (
                lax.dynamic_index_in_dim(held, v, 1, keepdims=False).reshape(-1, size_r) for v in (1 - mine, mine)
            )
    rest = kept_r

    final = tie(back[1][1], back_blocks)
    early_r = plan.first_send(dot_nn(x_sent, final).astype(bf16), True)
    kept_x1 = lax.optimization_barrier(dot_nn(x_kept, final))
    next_r, held_r, late_r = plan.next_sums(kept_x1 + tie(early_r, back_blocks).astype(f32), True)
    late_r = held_r + late_r.astype(f32)
    grad_z, grad_out = plan.slot_total(zo_sums)
    grad_out = grad_out.T
    input_grad = cotangent.astype(f32) + plan.pieces_of_batch(got_back).astype(f32)

    beyond = wide // shares
    parts = [rest[:beyond]] + [
        jnp.where(flip, rest[beyond + (1 - j) * heads : beyond + (2 - j) * heads], rest[beyond + j * heads : beyond + (j + 1) * heads])
        for j in two
    ]
    rest = jnp.concatenate(parts, axis=0).astype(bf16)
    half = size_r // 2
    columns = rest.shape[0]
    rests, smalls = [], []
    for e in range(shares):
        rows_e = lax.dynamic_slice_in_dim(rest, ((plan.share ^ e) // plan.k) * half, half, 1)
        rests.append(plan.across(rows_e, e) if e else rows_e)
        smalls.append(plan.across(small, e) if e else small)
    rests = side_by_side(jnp.concatenate(order_by_xor(rests, plan.share), axis=0), width)
    smalls = order_by_xor(smalls, plan.share)
    shared = sum(v[2 * count :] for v in smalls)
    smalls = jnp.stack([
        jnp.concatenate([smalls[i // 2][(i % 2) * count : (i % 2 + 1) * count], shared], axis=0) for i in range(tensor)
    ])
    cells = rests.shape[0]
    rests = jnp.broadcast_to(rests[None], (tensor, cells, width))
    last = jnp.concatenate([rests] + thirds(smalls), axis=1)
    last = tie(last, next_r)
    x1_sums = plan.slot_sends(plan.slot_blocks([tie(late_r, last)]), (1,))
    last = lax.all_to_all(tie(last, got_back), "t", 0, 0, tiled=True).reshape(tensor, -1, width)
    grad_x = plan.slot_total(tie(x0_sums + x1_sums, last))
    rests = one_by_one(jnp.sum(last[:, :cells].astype(f32), axis=0), half)
    rests = [rests[i * columns : (i + 1) * columns] for i in range(shares)]
    grad_bc = jnp.concatenate([v[:beyond] for v in rests], axis=0).T
    dts = [v[beyond + j * heads : beyond + (j + 1) * heads] for v in rests for j in two]
    grad_dt = lax.dynamic_index_in_dim(jnp.stack(dts), plan.t, 0, keepdims=False).T
    g_conv, g_conv_bias, g_gain, g_step, g_decay, g_skip, g_norm, g_conv_bc, g_conv_bc_bias = finish_step(
        where, last, cells, model, wide, heads
    )
    return (
        output, input_grad, g_norm, grad_z, grad_x, grad_bc, grad_dt, g_conv, g_conv_bias, g_conv_bc, g_conv_bc_bias,
        g_step, g_decay, g_skip, g_gain, grad_out,
    )


def solution(mesh):
    data, tensor = mesh.shape["dp"], mesh.shape["tensor"]
    groups = data // 2
    fine = Mesh(mesh.devices.reshape(groups, 2, tensor), AXES)
    dp = ("g", "c")

    def step(*args):
        return per_device(groups, tensor, *args)

    return jax.shard_map(
        step,
        mesh=fine,
        in_specs=(
            P(dp, None, "t"), P(dp, None), P(dp, None, "t"), P(), P(None, "t"), P(None, "t"), P(), P(None, "t"),
            P(None, "t"), P("t"), P(), P(), P("t"), P("t"), P("t"), P("t"), P("t", None),
        ),
        out_specs=(
            P(dp, None, "t"), P(dp, None, "t"), P("t"), P(dp, "t"), P(dp, "t"), P(dp, None), P(dp, "t"),
            P(None, "t"), P("t"), P(), P(), P("t"), P("t"), P("t"), P("t"), P("t", dp),
        ),
        check_vma=False,
    )
```

```python
import functools

import jax
import jax.numpy as jnp
from jax import lax
from jax.experimental import pallas as pl
from jax.experimental.layout import Layout, with_layout_constraint
from jax.experimental.pallas import tpu as pltpu
from jax.sharding import Mesh
from jax.sharding import PartitionSpec as P

SPAN = 256
HEAD = 64
LANES = 128
LOG2E = 1.4426950408889634
FAR = -1e30
bf16 = jnp.bfloat16
f32 = jnp.float32


def dot_nn(a, b):
    return lax.dot_general(a, b, (((1,), (0,)), ((), ())), preferred_element_type=f32)


def dot_nt(a, b):
    return lax.dot_general(a, b, (((1,), (1,)), ((), ())), preferred_element_type=f32)


def dot_tn(a, b):
    return lax.dot_general(a, b, (((0,), (0,)), ((), ())), preferred_element_type=f32)


def split_dot(a, b, flip=False):
    one = a.astype(bf16)
    two = (a - one.astype(f32)).astype(bf16)
    if flip:
        return dot_nn(b, one) + dot_nn(b, two)
    return dot_nn(one, b) + dot_nn(two, b)


def conv_terms(scr, block, halo, masks):
    span = block.shape[0]
    scr[0:8, :] = halo
    scr[8 : 8 + span, :] = block
    return [block] + [scr[8 - k : 8 - k + span, :] * masks(1 + k) for k in (1, 2, 3)]


def conv_sum(terms, weights, bias):
    total = bias + weights[3:4] * terms[0]
    for k in (1, 2, 3):
        total = total + weights[3 - k : 4 - k] * terms[k]
    return total


def sigmoid(v):
    return 0.5 + 0.5 * jnp.tanh(0.5 * v)


def lanes_of(columns, pair, low):
    return jnp.where(low, columns[:, 2 * pair : 2 * pair + 1], columns[:, 2 * pair + 1 : 2 * pair + 2])


def steps_of(pre, rate, lower, upper):
    dt = jnp.maximum(pre, 0.0) + jnp.log1p(jnp.exp(-jnp.abs(pre)))
    decay = dt * (rate * LOG2E)
    cum, cum_t = None, None
    for _ in range(3):
        part = decay.astype(bf16)
        decay = decay - part.astype(f32)
        one, two = dot_nn(lower, part), dot_tn(part, upper)
        cum, cum_t = (one, two) if cum is None else (cum + one, cum_t + two)
    return dt, cum, cum_t


def forward_kernel(
    v_ref, vh_ref, bc_ref, bch_ref, pre_ref, rate_ref, aux_ref, segc_ref, segr_ref,
    cw_ref, cb_ref, cwb_ref, cbb_ref, skip_ref,
    y_ref, hprev_ref, steps_ref, cumt_ref, state, scr, scrb, far_ref, mask_ref,
):
    span = v_ref.shape[0]
    pairs = v_ref.shape[1] // LANES
    n = bc_ref.shape[1] // 2

    @pl.when(pl.program_id(0) == 0)
    def _():
        state[...] = jnp.zeros_like(state)

    aux = aux_ref[...]
    for i in range(5):
        mask_ref[i] = jnp.broadcast_to(aux[:, i : i + 1], (span, LANES))
    bc_act = conv_sum(conv_terms(scrb, bc_ref[...], bch_ref[...], lambda i: aux[:, i : i + 1]), cwb_ref[...], cbb_ref[...])
    bc_act = bc_act * sigmoid(bc_act)
    b_mat = bc_act[:, :n].astype(bf16)
    c_mat = bc_act[:, n:].astype(bf16)
    scores = dot_nt(c_mat, b_mat)
    later = lax.broadcasted_iota(jnp.int32, (span, span), 0)
    earlier = lax.broadcasted_iota(jnp.int32, (span, span), 1)
    lower = (later >= earlier).astype(f32).astype(bf16)
    upper = (earlier >= later).astype(f32).astype(bf16)
    dt, cum, cum_t = steps_of(pre_ref[...], rate_ref[...], lower, upper)
    far_ref[...] = jnp.where((segc_ref[...] == segr_ref[...]) & (later >= earlier), 0.0, FAR)
    low = lax.broadcasted_iota(jnp.int32, (1, LANES), 1) < HEAD
    steps_ref[...] = jnp.concatenate([dt, cum, sigmoid(pre_ref[...])], axis=1)
    cumt_ref[...] = cum_t
    half = span // 2
    for p in range(pairs):
        sl = slice(p * LANES, (p + 1) * LANES)
        act = conv_sum(conv_terms(scr, v_ref[:, sl], vh_ref[:, sl], lambda i: mask_ref[i]), cw_ref[:, sl], cb_ref[:, sl])
        x = act * sigmoid(act)
        v = (x * lanes_of(dt, p, low)).astype(bf16)
        inside = None
        for e in (0, 1):
            h = 2 * p + e
            mine = jnp.where(low if e == 0 else ~low, v, jnp.zeros_like(v))
            part = []
            for rows, columns in ((slice(0, half), slice(0, half)), (slice(half, span), slice(0, span))):
                spread = (cum[rows, h : h + 1] - cum_t[h : h + 1, columns]) + far_ref[rows, columns]
                mixing = (scores[rows, columns] * jnp.exp2(spread)).astype(bf16)
                part.append(dot_nn(mixing, mine[columns]))
            part = jnp.concatenate(part, axis=0)
            inside = part if inside is None else inside + part
        wide_cum = lanes_of(cum, p, low)
        enter = jnp.exp2(wide_cum) * mask_ref[0]
        tail = jnp.exp2(wide_cum[span - 1 : span] - wide_cum) * mask_ref[1]
        prior = state[:, sl]
        low_prior = prior.astype(bf16)
        hprev_ref[0, :, sl] = low_prior
        outside = dot_nn(c_mat, low_prior) * enter
        y_ref[:, sl] = inside + outside + skip_ref[:, sl] * x
        weighted = (tail * v.astype(f32)).astype(bf16)
        state[:, sl] = enter[span - 1 : span] * prior + dot_tn(b_mat, weighted)


def backward_kernel(
    first, more, shares, where_ref,
    v_ref, vh_ref, bc_ref, bch_ref, steps_ref, rate_ref, aux_ref, segc_ref, segr_ref,
    cw_ref, cb_ref, cwb_ref, cbb_ref, skip_ref, cumt_ref, y_ref, dy_ref, hprev_ref, *rest,
):
    if more:
        before_refs, rest = rest[:shares], rest[shares:]
    dbc_refs, rest = rest[:shares], rest[shares:]
    (
        dv_ref, ddelta_ref, gx_ref, gbc_ref, gh_ref,
        dstate, after, afterb, scr, scrb, far_ref, dscore, dot_y, dot_x, last, tailed, entered, mask_ref,
    ) = rest
    span = v_ref.shape[0]
    channels = v_ref.shape[1]
    pairs = channels // LANES
    heads = channels // HEAD
    everyone = steps_ref.shape[1] // 3
    dt, cum, slope_dt = (steps_ref[:, i * everyone + first : i * everyone + first + heads] for i in range(3))
    rate = rate_ref[:, first : first + heads]
    half = span // 2
    n = bc_ref.shape[1] // 2

    @pl.when(pl.program_id(0) == 0)
    def _():
        for ref in (dstate, after, afterb, gx_ref, gbc_ref, gh_ref):
            ref[...] = jnp.zeros_like(ref)

    aux = aux_ref[...]
    for i in range(8):
        mask_ref[i] = jnp.broadcast_to(aux[:, i : i + 1], (span, LANES))
    terms_bc = conv_terms(scrb, bc_ref[...], bch_ref[...], lambda i: aux[:, i : i + 1])
    act_bc = conv_sum(terms_bc, cwb_ref[...], cbb_ref[...])
    sig_bc = sigmoid(act_bc)
    bc_act = act_bc * sig_bc
    b_mat = bc_act[:, :n].astype(bf16)
    c_mat = bc_act[:, n:].astype(bf16)
    scores = dot_nt(b_mat, c_mat)
    earlier = lax.broadcasted_iota(jnp.int32, (span, span), 0)
    later = lax.broadcasted_iota(jnp.int32, (span, span), 1)
    far_ref[...] = jnp.where((segc_ref[...] == segr_ref[...]) & (later >= earlier), 0.0, FAR)
    low = lax.broadcasted_iota(jnp.int32, (1, LANES), 1) < HEAD
    upper = (later >= earlier).astype(f32).astype(bf16)
    dscore[...] = jnp.zeros_like(dscore)

    def rows_of(value):
        return jnp.sum(value, axis=0, keepdims=True)

    for p in range(pairs):
        sl = slice(p * LANES, (p + 1) * LANES)
        terms = conv_terms(scr, v_ref[:, sl], vh_ref[:, sl], lambda i: mask_ref[i])
        act = conv_sum(terms, cw_ref[:, sl], cb_ref[:, sl])
        sig = sigmoid(act)
        x = act * sig
        dt_lanes = lanes_of(dt, p, low)
        v = (x * dt_lanes).astype(bf16)
        v_wide = v.astype(f32)
        dy = dy_ref[:, sl]
        dy_wide = dy.astype(f32)
        d_inside = None
        for e in (0, 1):
            h = 2 * p + e
            mask = low if e == 0 else ~low
            mine = jnp.where(mask, dy, jnp.zeros_like(dy))
            part = []
            for rows, columns in ((slice(0, half), slice(0, span)), (slice(half, span), slice(half, span))):
                spread = (cumt_ref[first + h : first + h + 1, columns] - cum[rows, h : h + 1]) + far_ref[rows, columns]
                kernel = jnp.exp2(spread)
                mixing = (scores[rows, columns] * kernel).astype(bf16)
                part.append(dot_nn(mixing, mine[columns]))
                dscore[rows, columns] += dot_nt(v[rows], mine[columns]) * kernel
            part = jnp.concatenate(part, axis=0)
            d_inside = part if d_inside is None else d_inside + part
        wide_cum = lanes_of(cum, p, low)
        enter = jnp.exp2(wide_cum) * mask_ref[0]
        tail = jnp.exp2(wide_cum[span - 1 : span] - wide_cum) * mask_ref[1]
        d_new = dstate[:, sl]
        low_new = d_new.astype(bf16)
        d_outer = dot_nn(b_mat, low_new) * tail
        dval = d_inside + d_outer
        skip = skip_ref[:, sl]
        dot_y[:, sl] = dy_wide * (y_ref[:, sl] - skip * x) - v_wide * dval
        dot_x[:, sl] = x * dval
        entering = (enter * dy_wide).astype(bf16)
        entered[:, sl] = entering
        tailed[:, sl] = (tail * v_wide).astype(bf16)
        prior = hprev_ref[0, :, sl]
        carried = enter[span - 1 : span]
        last[:, sl] = rows_of(v_wide * d_outer) + carried * rows_of(prior.astype(f32) * d_new)
        dx = dt_lanes * dval + skip * dy_wide
        dconv = dx * (sig * (1.0 + act * (1.0 - sig)))
        scr[0:span, :] = dconv
        scr[span : span + 8, :] = after[:, sl]
        d_pre = cw_ref[3:4, sl] * dconv
        for k in (1, 2, 3):
            d_pre = d_pre + cw_ref[3 - k : 4 - k, sl] * (scr[k : k + span, :] * mask_ref[4 + k])
        dv_ref[:, sl] = d_pre.astype(bf16)
        after[:, sl] = dconv[0:8]
        for k in (0, 1, 2, 3):
            gx_ref[3 - k : 4 - k, sl] += rows_of(dconv * terms[k])
        gx_ref[4:5, sl] += rows_of(dconv)
        gx_ref[5:6, sl] += rows_of(dy_wide * x)

    ds = dscore[...].astype(bf16)
    d_b = dot_nn(ds, c_mat) + dot_nt(tailed[...], dstate[...].astype(bf16))
    d_c = dot_tn(ds, b_mat) + dot_nt(entered[...], hprev_ref[0])
    slope = sig_bc * (1.0 + act_bc * (1.0 - sig_bc))
    dconv_bc = jnp.concatenate([d_b, d_c], axis=1) * slope
    scrb[0:span, :] = dconv_bc
    scrb[span : span + 8, :] = afterb[...]
    d_pre = cwb_ref[3:4] * dconv_bc
    for k in (1, 2, 3):
        d_pre = d_pre + cwb_ref[3 - k : 4 - k] * (scrb[k : k + span, :] * aux[:, 4 + k : 5 + k])
    cut = 2 * n // shares
    pieces = [d_pre[:, s * cut : (s + 1) * cut] for s in range(shares)]
    own = jnp.full((span, cut), where_ref[0], jnp.int32)
    bit = 1
    while bit < shares:
        pieces = [jnp.where((own & bit) != 0, pieces[s ^ bit], pieces[s]) for s in range(shares)]
        bit *= 2
    for e in range(shares):
        dbc_refs[e][...] = pieces[e] + before_refs[e][...] if more else pieces[e]
    afterb[...] = dconv_bc[0:8]
    for k in (0, 1, 2, 3):
        gbc_ref[3 - k : 4 - k] += rows_of(dconv_bc * terms_bc[k])
    gbc_ref[4:5] += rows_of(dconv_bc)

    for p in range(pairs):
        sl = slice(p * LANES, (p + 1) * LANES)
        carried = jnp.exp2(lanes_of(cum[span - 1 : span], p, low)) * aux[span - 1 : span, 0:1]
        dstate[:, sl] = carried * dstate[:, sl] + dot_tn(c_mat, entered[:, sl])

    place = lax.broadcasted_iota(jnp.int32, (channels, heads), 0) // HEAD
    head = lax.broadcasted_iota(jnp.int32, (channels, heads), 1)
    select = (place == head).astype(bf16)
    d_cum = split_dot(dot_y[...], select)
    final = split_dot(jnp.broadcast_to(last[...], (8, channels)), select)[0:1]
    row = lax.broadcasted_iota(jnp.int32, (span, heads), 0)
    d_cum = d_cum + jnp.where(row == span - 1, final, 0.0)
    d_decay = split_dot(d_cum, upper, flip=True)
    d_dt = split_dot(dot_x[...], select) + d_decay * rate
    d_delta = d_dt * slope_dt
    ddelta_ref[...] = d_delta.astype(bf16)
    gh_ref[0:1] += rows_of(d_delta)
    gh_ref[1:2] += rows_of(d_decay * dt * rate)


def scan_specs(common, width, column, reverse):
    length, channels = common[0].shape
    wide, heads = common[1].shape[1], common[2].shape[1]
    blocks = length // SPAN
    tall = SPAN // 8

    def at(b):
        return blocks - 1 - b if reverse else b

    def rows(size, at_column=0):
        return pl.BlockSpec((SPAN, size), lambda b, *_: (at(b), at_column))

    def halo(size, at_column=0):
        return pl.BlockSpec((8, size), lambda b, *_: (jnp.maximum(at(b) * tall - 1, 0), at_column))

    def whole(shape, at_column=0):
        return pl.BlockSpec(shape, lambda b, *_: (0, at_column))

    states = pl.BlockSpec((1, wide // 2, width), lambda b, *_: (at(b), 0, column))
    ins = [
        rows(width, column), halo(width, column), rows(wide), halo(wide), rows(heads), whole((1, heads)), rows(8), rows(1),
        pl.BlockSpec((1, SPAN), lambda b, *_: (0, at(b))),
        whole((4, width), column), whole((1, width), column), whole((4, wide)), whole((1, wide)),
        whole((1, width), column),
    ]
    return blocks, rows, whole, states, ins


def forward_scan(common):
    v_pre, bc_pre, pre = common[:3]
    length, channels = v_pre.shape
    wide, heads = bc_pre.shape[1], pre.shape[1]
    blocks, rows, whole, states, ins = scan_specs(common, channels, 0, False)
    return pl.pallas_call(
        forward_kernel,
        grid=(blocks,),
        in_specs=ins,
        out_specs=[rows(channels), states, rows(3 * heads), pl.BlockSpec((heads, SPAN), lambda b: (0, b))],
        out_shape=[
            jax.ShapeDtypeStruct((length, channels), f32),
            jax.ShapeDtypeStruct((blocks, wide // 2, channels), bf16),
            jax.ShapeDtypeStruct((length, 3 * heads), f32), jax.ShapeDtypeStruct((heads, length), f32),
        ],
        scratch_shapes=[
            pltpu.VMEM((wide // 2, channels), f32), pltpu.VMEM((SPAN + 8, LANES), f32),
            pltpu.VMEM((SPAN + 8, wide), f32), pltpu.VMEM((SPAN, SPAN), f32), pltpu.VMEM((5, SPAN, LANES), f32),
        ],
        compiler_params=pltpu.CompilerParams(vmem_limit_bytes=20 * 2**20),
        cost_estimate=pl.CostEstimate(flops=channels * length, bytes_accessed=channels * length, transcendentals=0),
    )(v_pre, v_pre, bc_pre, bc_pre, *common[2:])


def backward_scan(common, half, shares, where, steps, cum_t, y, dy, hprev, before=()):
    v_pre, bc_pre, pre = common[:3]
    length, channels = v_pre.shape[0], v_pre.shape[1] // 2
    wide, heads = bc_pre.shape[1], pre.shape[1] // 2
    blocks, rows, whole, states, ins = scan_specs(common, channels, half, True)
    split = rows(wide // shares)
    ins[4] = rows(steps.shape[1])
    sums = pl.BlockSpec((2 * heads, SPAN), lambda b, *_: (0, blocks - 1 - b))
    out = pl.pallas_call(
        functools.partial(backward_kernel, half * heads, bool(before), shares),
        grid_spec=pltpu.PrefetchScalarGridSpec(
            num_scalar_prefetch=1,
            grid=(blocks,),
            in_specs=ins + [sums, rows(channels, half), rows(channels, half), states] + [split] * len(before),
            out_specs=[split] * shares
            + [rows(channels), rows(heads), whole((8, channels)), whole((8, wide)), whole((8, heads))],
            scratch_shapes=[
                pltpu.VMEM((wide // 2, channels), f32), pltpu.VMEM((8, channels), f32), pltpu.VMEM((8, wide), f32),
                pltpu.VMEM((SPAN + 8, LANES), f32), pltpu.VMEM((SPAN + 8, wide), f32), pltpu.VMEM((SPAN, SPAN), f32),
                pltpu.VMEM((SPAN, SPAN), f32), pltpu.VMEM((SPAN, channels), f32), pltpu.VMEM((SPAN, channels), f32),
                pltpu.VMEM((1, channels), f32), pltpu.VMEM((SPAN, channels), bf16), pltpu.VMEM((SPAN, channels), bf16),
                pltpu.VMEM((8, SPAN, LANES), f32),
            ],
        ),
        out_shape=[jax.ShapeDtypeStruct((length, wide // shares), f32)] * shares
        + [
            jax.ShapeDtypeStruct((length, channels), bf16), jax.ShapeDtypeStruct((length, heads), bf16),
            jax.ShapeDtypeStruct((8, channels), f32), jax.ShapeDtypeStruct((8, wide), f32),
            jax.ShapeDtypeStruct((8, heads), f32),
        ],
        compiler_params=pltpu.CompilerParams(vmem_limit_bytes=56 * 2**20),
        cost_estimate=pl.CostEstimate(flops=channels * length, bytes_accessed=channels * length, transcendentals=0),
    )(where, v_pre, v_pre, bc_pre, bc_pre, steps, *common[3:], cum_t, y, dy, hprev, *before)
    return tuple(out[:shares]), *out[shares:]


def assemble(moves, index, sources, shape):
    def kernel(index_ref, *refs):
        out_ref = refs[-1]
        at = index_ref[0]
        for source, lead, rows, base, stride, offset, columns in moves:
            start = pl.multiple_of(base + (at ^ offset) * stride, stride)
            out_ref[pl.ds(start, rows.stop - rows.start), columns] = refs[source][(*lead, rows, slice(None))]

    return pl.pallas_call(
        kernel,
        grid_spec=pltpu.PrefetchScalarGridSpec(
            num_scalar_prefetch=1,
            grid=(1,),
            in_specs=[pl.BlockSpec(v.shape, lambda i, s, rank=v.ndim: (0,) * rank) for v in sources],
            out_specs=pl.BlockSpec(shape, lambda i, s: (0, 0)),
        ),
        out_shape=jax.ShapeDtypeStruct(shape, bf16),
        compiler_params=pltpu.CompilerParams(vmem_limit_bytes=10 * 2**20),
        cost_estimate=pl.CostEstimate(flops=0, bytes_accessed=4 * shape[0] * shape[1], transcendentals=0),
    )(index.reshape(1), *sources)


def rows_in_order(shares, blocks):
    each = blocks // shares

    def at(i, where_ref):
        return (where_ref[0] ^ (shares - 1 - i // each)) * each + i % each

    return each, at


def pick_part(shares, parts, cot):
    each = pl.num_programs(0) // shares
    for e in range(shares):
        @pl.when(pl.program_id(0) // each == shares - 1 - e)
        def _(e=e):
            cot[...] = parts[e][...]


def gate_kernel(shares, where_ref, normed_ref, wz_ref, y_ref, wo_ref, gain_ref, *refs):
    parts, (stats_ref, sent_ref, kept_ref, cot) = refs[:shares], refs[shares:]
    span, model = cot.shape
    pick_part(shares, parts, cot)
    half = model // 2
    sent_ref[...] = cot[:, pl.ds(pl.multiple_of((1 - where_ref[1]) * half, half), half)].T
    kept_ref[...] = cot[:, pl.ds(pl.multiple_of(where_ref[1] * half, half), half)].T
    gate = dot_nn(normed_ref[...], wz_ref[...])
    d_mixed = dot_nt(cot[...], wo_ref[...])
    gated = y_ref[...] * (gate * sigmoid(gate))
    squares = jnp.sum(gated * gated, axis=1, keepdims=True)
    product = jnp.sum(d_mixed * gain_ref[...] * gated, axis=1, keepdims=True)
    lane = lax.broadcasted_iota(jnp.int32, (span, LANES), 1)
    both = jnp.where(lane == 0, squares, jnp.where(lane == 1, product, 0.0))
    stats_ref[...] = both.T[0:8]


def norm_kernel(
    shares, inner, where_ref, normed_ref, wz_ref, y_ref, wo_ref, gain_ref, stats_ref, *refs
):
    parts, refs = refs[:shares], refs[shares:]
    mixed_ref, dy_ref, dgate_ref, ggain_ref, sent_ref, kept_ref, cot, gate_ref, dmix_ref = refs

    @pl.when(pl.program_id(0) == 0)
    def _():
        ggain_ref[...] = jnp.zeros_like(ggain_ref)

    pick_part(shares, parts, cot)
    gate_ref[...] = dot_nn(normed_ref[...], wz_ref[...])
    dmix_ref[...] = dot_nt(cot[...], wo_ref[...])
    stats = jnp.concatenate([stats_ref[...]] + [jnp.zeros((LANES - 8, stats_ref.shape[1]), f32)], axis=0).T
    scale = lax.rsqrt(stats[:, 0:1] * (1.0 / inner) + 1e-05)
    factor = scale * scale * scale * (stats[:, 1:2] * (1.0 / inner))
    for at in range(0, y_ref.shape[1], LANES):
        sl = slice(at, at + LANES)
        y, gate, gain = y_ref[:, sl], gate_ref[:, sl], gain_ref[:, sl]
        sig = sigmoid(gate)
        silu = gate * sig
        gated = y * silu
        scaled = dmix_ref[:, sl] * scale
        mixed_ref[:, sl] = (gated * scale * gain).astype(bf16)
        d_gated = scaled * gain - gated * factor
        dy_ref[:, sl] = (d_gated * silu).astype(bf16)
        dgate_ref[:, sl] = (d_gated * y * (sig + silu * (1.0 - sig))).astype(bf16)
        ggain_ref[0:1, sl] += jnp.sum(scaled * gated, axis=0, keepdims=True)
    result = dot_nn(mixed_ref[...], wo_ref[...])
    each = pl.num_programs(0) // shares

    @pl.when(pl.program_id(0) < (shares - 1) * each)
    def _():
        sent_ref[...] = result.astype(bf16)

    @pl.when(pl.program_id(0) >= (shares - 1) * each)
    def _():
        kept_ref[...] = result.astype(bf16)


def gated_specs(shares, normed, y):
    length, model = normed.shape
    channels = y.shape[1]
    blocks = length // SPAN
    each, at = rows_in_order(shares, blocks)

    def rows(size):
        return pl.BlockSpec((SPAN, size), lambda i, s: (at(i, s), 0))

    def whole(shape):
        return pl.BlockSpec(shape, lambda i, s: (0, 0))

    ins = [rows(model), whole((model, channels)), rows(channels), whole((channels, model)), whole((1, channels))]
    parts = [pl.BlockSpec((SPAN, model), lambda i, s: (i % each, 0))] * shares
    return blocks, each, at, rows, whole, ins, parts


def gate_step(shares, where, normed, w_z, y, w_out, gain, cot_parts):
    length, model = normed.shape
    channels = y.shape[1]
    blocks, each, at, rows, whole, ins, parts = gated_specs(shares, normed, y)
    tall = pl.BlockSpec((model // 2, SPAN), lambda i, s: (0, at(i, s)))
    return pl.pallas_call(
        functools.partial(gate_kernel, shares),
        grid_spec=pltpu.PrefetchScalarGridSpec(
            num_scalar_prefetch=1,
            grid=(blocks,),
            in_specs=ins + parts,
            out_specs=[pl.BlockSpec((8, SPAN), lambda i, s: (0, at(i, s))), tall, tall],
            scratch_shapes=[pltpu.VMEM((SPAN, model), bf16)],
        ),
        out_shape=[
            jax.ShapeDtypeStruct((8, length), f32), jax.ShapeDtypeStruct((model // 2, length), bf16),
            jax.ShapeDtypeStruct((model // 2, length), bf16),
        ],
        compiler_params=pltpu.CompilerParams(vmem_limit_bytes=20 * 2**20),
        cost_estimate=pl.CostEstimate(flops=4 * length * model * channels, bytes_accessed=8 * length * channels, transcendentals=0),
    )(where, normed, w_z, y, w_out, gain, *cot_parts)


def norm_step(shares, inner, where, normed, w_z, y, w_out, gain, stats, cot_parts):
    length, model = normed.shape
    channels = y.shape[1]
    blocks, each, at, rows, whole, ins, parts = gated_specs(shares, normed, y)
    many = (shares - 1) * each
    return pl.pallas_call(
        functools.partial(norm_kernel, shares, inner),
        grid_spec=pltpu.PrefetchScalarGridSpec(
            num_scalar_prefetch=1,
            grid=(blocks,),
            in_specs=ins + [pl.BlockSpec((8, SPAN), lambda i, s: (0, at(i, s)))] + parts,
            out_specs=[
                rows(channels), rows(channels), rows(channels), whole((8, channels)),
                pl.BlockSpec((SPAN, model), lambda i, s: (jnp.minimum(i, many - 1), 0)),
                pl.BlockSpec((SPAN, model), lambda i, s: (jnp.maximum(i - many, 0), 0)),
            ],
            scratch_shapes=[
                pltpu.VMEM((SPAN, model), bf16), pltpu.VMEM((SPAN, channels), f32), pltpu.VMEM((SPAN, channels), f32)
            ],
        ),
        out_shape=[jax.ShapeDtypeStruct((length, channels), bf16)] * 3
        + [
            jax.ShapeDtypeStruct((8, channels), f32), jax.ShapeDtypeStruct((many * SPAN, model), bf16),
            jax.ShapeDtypeStruct((each * SPAN, model), bf16),
        ],
        compiler_params=pltpu.CompilerParams(vmem_limit_bytes=26 * 2**20),
        cost_estimate=pl.CostEstimate(flops=6 * length * model * channels, bytes_accessed=18 * length * channels, transcendentals=0),
    )(where, normed, w_z, y, w_out, gain, stats, *cot_parts)


def cut_kernel(size, where_ref, source_ref, sent_ref, kept_ref, turned):
    turned[...] = source_ref[...].T
    for i in range(sent_ref.shape[0] // size):
        to = slice(i * size, (i + 1) * size)
        sent_ref[to] = turned[pl.ds(pl.multiple_of((2 * i + 1 - where_ref[2]) * size, size), size)]
        kept_ref[to] = turned[pl.ds(pl.multiple_of((2 * i + where_ref[2]) * size, size), size)]


def cut_step(groups, where, source):
    length, model = source.shape
    out = pl.BlockSpec((model // 2, length), lambda i, s: (0, 0))
    return pl.pallas_call(
        functools.partial(cut_kernel, model // groups),
        grid_spec=pltpu.PrefetchScalarGridSpec(
            num_scalar_prefetch=1,
            grid=(1,),
            in_specs=[pl.BlockSpec((length, model), lambda i, s: (0, 0))],
            out_specs=[out, out],
            scratch_shapes=[pltpu.VMEM((model, length), bf16)],
        ),
        out_shape=[jax.ShapeDtypeStruct((model // 2, length), bf16)] * 2,
        compiler_params=pltpu.CompilerParams(vmem_limit_bytes=14 * 2**20),
        cost_estimate=pl.CostEstimate(flops=0, bytes_accessed=4 * length * model, transcendentals=0),
    )(where, source)


def base_kernel(gate_ref, wz_ref, value_ref, wx_ref, out_ref):
    out_ref[...] = (dot_nt(gate_ref[...], wz_ref[...]) + dot_nt(value_ref[...], wx_ref[...])).astype(bf16)


def base_step(d_gate, w_z, d_value, w_x):
    length, channels = d_gate.shape
    model = w_z.shape[0]
    width = d_value.shape[1]

    def rows(size):
        return pl.BlockSpec((SPAN, size), lambda b: (b, 0))

    return pl.pallas_call(
        base_kernel,
        grid=(length // SPAN,),
        in_specs=[
            rows(channels), pl.BlockSpec((model, channels), lambda b: (0, 0)), rows(width),
            pl.BlockSpec((model, width), lambda b: (0, 0)),
        ],
        out_specs=rows(model),
        out_shape=jax.ShapeDtypeStruct((length, model), bf16),
        compiler_params=pltpu.CompilerParams(vmem_limit_bytes=56 * 2**20),
        cost_estimate=pl.CostEstimate(flops=3 * length * channels * model, bytes_accessed=8 * length * channels, transcendentals=0),
    )(d_gate, w_z, d_value, w_x)


def last_kernel(shares, where_ref, *refs):
    own, parts, refs = refs[:shares], refs[shares : 2 * shares], refs[2 * shares :]
    dv_ref, one_ref, two_ref, base_ref, wx_ref, wb_ref, wd_ref, sent_ref, kept_ref, low_ref, gain_ref, u_ref = refs

    @pl.when(pl.program_id(0) == 0)
    def _():
        gain_ref[...] = jnp.zeros_like(gain_ref)

    pick_part(shares, parts, u_ref)
    low = own[0][...]
    for ref in own[1:]:
        low = low + ref[...]
    low = low.astype(bf16)
    low_ref[...] = low
    steps = jnp.concatenate([one_ref[...].astype(f32), two_ref[...].astype(f32)], axis=1).astype(bf16)
    total = dot_nt(dv_ref[...], wx_ref[...]) + dot_nt(low, wb_ref[...]) + dot_nn(steps, wd_ref[...])
    total = total + base_ref[...].astype(f32)
    u = u_ref[...].astype(f32)
    scale = lax.rsqrt(jnp.sum(u * u, axis=1, keepdims=True) * (1.0 / u.shape[1]) + 1e-05)
    gain_ref[0:1] += jnp.sum(total * (u * scale), axis=0, keepdims=True)
    each = pl.num_programs(0) // shares

    @pl.when(pl.program_id(0) < (shares - 1) * each)
    def _():
        sent_ref[...] = total.astype(bf16)

    @pl.when(pl.program_id(0) >= (shares - 1) * each)
    def _():
        kept_ref[...] = total.astype(bf16)


def last_step(shares, where, d_bcs, u_parts, d_value, steps, base, w_x, share_bc, w_dt):
    length, width = d_value.shape
    model = base.shape[1]
    blocks = length // SPAN
    each, at = rows_in_order(shares, blocks)

    def rows(size):
        return pl.BlockSpec((SPAN, size), lambda i, s: (at(i, s), 0))

    def whole(value):
        return pl.BlockSpec(value.shape, lambda i, s: (0, 0))

    many = (shares - 1) * each
    narrow = d_bcs[0].shape[1]
    return pl.pallas_call(
        functools.partial(last_kernel, shares),
        grid_spec=pltpu.PrefetchScalarGridSpec(
            num_scalar_prefetch=1,
            grid=(blocks,),
            in_specs=[rows(narrow)] * shares
            + [pl.BlockSpec((SPAN, model), lambda i, s: (i % each, 0))] * shares
            + [rows(width), rows(steps[0].shape[1]), rows(steps[1].shape[1]), rows(model)]
            + [pl.BlockSpec((model, width), lambda i, s: (0, 1)), whole(share_bc), whole(w_dt)],
            out_specs=[
                pl.BlockSpec((SPAN, model), lambda i, s: (jnp.minimum(i, many - 1), 0)),
                pl.BlockSpec((SPAN, model), lambda i, s: (jnp.maximum(i - many, 0), 0)),
                rows(narrow),
                pl.BlockSpec((8, model), lambda i, s: (0, 0)),
            ],
            scratch_shapes=[pltpu.VMEM((SPAN, model), bf16)],
        ),
        out_shape=[
            jax.ShapeDtypeStruct((many * SPAN, model), bf16), jax.ShapeDtypeStruct((each * SPAN, model), bf16),
            jax.ShapeDtypeStruct((length, narrow), bf16), jax.ShapeDtypeStruct((8, model), f32),
        ],
        compiler_params=pltpu.CompilerParams(vmem_limit_bytes=56 * 2**20),
        cost_estimate=pl.CostEstimate(flops=2 * length * width * model, bytes_accessed=8 * length * model, transcendentals=0),
    )(where, *d_bcs, *u_parts, d_value, *steps, base, w_x, share_bc, w_dt)


def input_kernel(tensor, *refs):
    parts, (u_ref, gain_ref, out_ref) = refs[:-3], refs[-3:]
    d_part = parts[0][...].astype(f32)
    for ref in parts[1:]:
        d_part = d_part + ref[...].astype(f32)
    u = u_ref[...].astype(f32)
    model = u.shape[1]
    scale = lax.rsqrt(jnp.sum(u * u, axis=1, keepdims=True) * (1.0 / model) + 1e-05)
    weighted = d_part * gain_ref[...]
    dot = jnp.sum(weighted * u, axis=1, keepdims=True)
    d_input = (scale * weighted - u * (scale * scale * scale * (dot * (1.0 / model)))).astype(bf16)
    width = model // tensor
    for i in range(tensor):
        out_ref[i] = d_input[:, i * width : (i + 1) * width]


def input_step(tensor, parts, u_part, norm_gain):
    rows_in, model = u_part.shape
    rows = pl.BlockSpec((SPAN, model), lambda b: (b, 0))
    return pl.pallas_call(
        functools.partial(input_kernel, tensor),
        grid=(rows_in // SPAN,),
        in_specs=[rows] * (len(parts) + 1) + [pl.BlockSpec((1, model), lambda b: (0, 0))],
        out_specs=pl.BlockSpec((tensor, SPAN, model // tensor), lambda b: (0, b, 0)),
        out_shape=jax.ShapeDtypeStruct((tensor, rows_in, model // tensor), bf16),
        compiler_params=pltpu.CompilerParams(vmem_limit_bytes=10 * 2**20),
        cost_estimate=pl.CostEstimate(flops=10 * rows_in * model, bytes_accessed=10 * rows_in * model, transcendentals=0),
    )(*parts, u_part, norm_gain)


def finish_kernel(tensor, model, wide, heads, cells, where_ref, last_ref, *out_refs):
    width = last_ref.shape[2]
    lines = (last_ref.shape[1] - cells) // 3
    parts = None
    for i in range(tensor):
        for n in (2, 1, 0):
            piece = last_ref[i, cells + n * lines : cells + (n + 1) * lines].astype(f32)
            parts = piece if parts is None else parts + piece
    conv_ref, bias_ref, gain_ref, step_ref, decay_ref, skip_ref, norm_ref, bc_ref, bc_bias_ref = out_refs
    conv_ref[...] = parts[0:4]
    bias_ref[...] = parts[4]
    gain_ref[...] = parts[5]
    for n, ref in enumerate((step_ref, decay_ref, skip_ref)):
        ref[...] = parts[6, n * heads : (n + 1) * heads]

    def shared(start, size):
        return parts[7 + start // width, start % width : start % width + size]

    size = model // tensor
    norm = shared(0, size)
    at = jnp.full((size,), where_ref[3], jnp.int32)
    for i in range(1, tensor):
        norm = jnp.where(at == i, shared(i * size, size), norm)
    norm_ref[...] = norm
    for n in range(4):
        bc_ref[n] = shared(model + n * wide, wide)
    bc_bias_ref[...] = shared(model + 4 * wide, wide)


def finish_step(where, last, cells, model, wide, heads):
    tensor, _, width = last.shape
    shapes = [(4, width), (width,), (width,), (heads,), (heads,), (heads,), (model // tensor,), (4, wide), (wide,)]
    return pl.pallas_call(
        functools.partial(finish_kernel, tensor, model, wide, heads, cells),
        grid_spec=pltpu.PrefetchScalarGridSpec(
            num_scalar_prefetch=1,
            grid=(1,),
            in_specs=[pl.BlockSpec(last.shape, lambda i, s: (0, 0, 0))],
            out_specs=[pl.BlockSpec(v, lambda i, s, rank=len(v): (0,) * rank) for v in shapes],
        ),
        out_shape=[jax.ShapeDtypeStruct(v, f32) for v in shapes],
        compiler_params=pltpu.CompilerParams(vmem_limit_bytes=6 * 2**20),
    )(where, last)


EPS = 1e-05
AXES = ("g", "c", "t")


def tie(value, *others):
    return lax.optimization_barrier((value, *others))[0]


def row_major(value):
    return with_layout_constraint(value, Layout(major_to_minor=tuple(range(value.ndim))))


def thirds(value):
    parts = []
    for _ in range(3):
        part = lax.reduce_precision(value, 8, 7)
        parts.append(part.astype(bf16))
        value = value - part
    return parts


def side_by_side(value, width):
    each = width // value.shape[1]
    rows = value.shape[0] // each
    return jnp.concatenate([value[i * rows : (i + 1) * rows] for i in range(each)], axis=1)


def one_by_one(value, width):
    return jnp.concatenate([value[:, i : i + width] for i in range(0, value.shape[1], width)], axis=0)


def order_by_xor(pieces, index):
    bit = 1
    while bit < len(pieces):
        flip = (index & bit) != 0
        pieces = [jnp.where(flip, pieces[i ^ bit], pieces[i]) for i in range(len(pieces))]
        bit *= 2
    return pieces


class Plan:
    def __init__(self, groups, tensor, per_dp):
        self.groups, self.tensor, self.per_dp = groups, tensor, per_dp
        self.k = tensor // (2 * per_dp)
        self.shares = 2 * self.k
        self.seqs = 2 * per_dp
        self.t = lax.axis_index("t")
        self.c = lax.axis_index("c")
        self.g = lax.axis_index("g")
        self.seq = self.t // self.k
        self.share = self.c * self.k + self.t % self.k
        self.piece = (self.seq % per_dp) * self.shares + self.share
        self.bits = [1 << b for b in range(groups.bit_length() - 1)]

    def send(self, value, where):
        def number(g, c, t):
            return (g * 2 + c) * self.tensor + t

        pairs = [
            (number(g, c, t), number(*where(g, c, t)))
            for g in range(self.groups) for c in range(2) for t in range(self.tensor)
        ]
        return lax.ppermute(value, AXES, pairs)

    def across(self, value, e):
        k = self.k

        def where(g, c, t):
            other = (c * k + t % k) ^ e
            return g, other // k, t // k * k + other % k

        return self.send(value, where)

    def around(self, value, e):
        return self.send(value, lambda g, c, t: (g ^ e, c, t))

    def along(self, value, e):
        return self.send(value, lambda g, c, t: (g, c, t ^ (e * self.k)))

    def swap_for_sequence(self, sources):
        per_dp, length, width = sources[0].shape
        halves = [v.reshape(per_dp, 2, length // 2, width) for v in sources]
        sent = jnp.stack([lax.dynamic_index_in_dim(v, 1 - self.c, 1, keepdims=False) for v in halves])
        got = self.send(sent, lambda g, c, t: (g, 1 - c, t))
        out = []
        for i, v in enumerate(halves):
            kept = lax.dynamic_index_in_dim(v, self.c, 1, keepdims=False)
            out.append(jnp.concatenate(order_by_xor([kept, got[i]], self.c), axis=0))
        return out

    def to_sequence(self, source):
        seqs, rows, width = source.shape
        return lax.all_to_all(source.reshape(self.tensor, rows // self.k, width), "t", 0, 0, tiled=True)

    def pieces_of_sequence(self, got):
        return jnp.concatenate([got[i] for i in range(self.tensor)], axis=1)

    def blocks_back(self, source):
        width = source.shape[1] // self.tensor
        return jnp.stack([source[:, i * width : (i + 1) * width] for i in range(self.tensor)])

    def from_sequence(self, blocks):
        got = lax.all_to_all(blocks, "t", 0, 0, tiled=True)
        return got.reshape(self.seqs, self.k * blocks.shape[1], blocks.shape[2])

    def pieces_of_batch(self, got):
        per_dp = self.per_dp
        kept = lax.dynamic_slice_in_dim(got, self.c * per_dp, per_dp, 0)
        sent = lax.dynamic_slice_in_dim(got, (1 - self.c) * per_dp, per_dp, 0)
        other = self.send(sent, lambda g, c, t: (g, 1 - c, t))
        return jnp.concatenate(order_by_xor([kept, other], self.c), axis=1), other

    def gather_shares(self, part):
        got = [part] + [self.across(part, e) for e in range(1, self.shares)]
        return jnp.concatenate(order_by_xor(got, self.share), axis=0)

    def sum_part(self, whole, axis, wire):
        size = whole.shape[axis] // self.shares
        total = lax.dynamic_slice_in_dim(whole, self.share * size, size, axis)
        for e in range(1, self.shares):
            other = lax.dynamic_slice_in_dim(whole, (self.share ^ e) * size, size, axis).astype(wire)
            total = total + self.across(other, e).astype(f32)
        return total

    def sum_shares(self, value):
        e = 1
        while e < self.shares:
            value = value + self.across(value, e)
            e *= 2
        return value

    def slot(self, value, j):
        def where(g, c, t):
            share = t // 2
            return g, share // self.k, (2 * c + (j ^ (t & 1))) * self.k + share % self.k

        return self.send(value, where)

    def unslot(self, value, j1, j0):
        def where(g, c, t):
            seq, share = t // self.k, c * self.k + t % self.k
            return g, j1 ^ (seq >> 1), 2 * share + (j0 ^ (seq & 1))

        return self.send(value, where)

    def slice_of(self, whole):
        size = whole.shape[0] // self.groups
        return lax.dynamic_slice_in_dim(whole, self.g * size, size, 0)

    def spread(self, piece, first, until=None):
        held = piece[None]
        bits = self.bits if first else self.bits[::-1]
        offsets = [0]
        for bit in bits:
            got = self.around(held, bit)
            more = [off | bit for off in offsets]
            if bit == bits[-1]:
                return [held, got if until is None else tie(got, until)], [offsets, more]
            held = jnp.concatenate([held, got], axis=0)
            offsets = offsets + more

    def halves(self, source, first):
        bit = self.bits[0] if first else self.bits[-1]
        size = source.shape[1] // self.groups
        own = self.g & bit
        out = []
        for at in (bit - own, own):
            blocks = [
                lax.dynamic_slice_in_dim(source, (r + at) * size, size, 1) for r in range(self.groups) if not r & bit
            ]
            out.append(jnp.concatenate(blocks, axis=1))
        return out

    def first_send(self, sent, first):
        return self.around(sent, self.bits[0] if first else self.bits[-1])

    def next_sums(self, held, first, after=()):
        bits = self.bits[1:] if first else self.bits[-2::-1]
        left = len(bits)
        held = held.reshape((2,) * left + (-1, held.shape[-1]))
        for bit in bits:
            axis = left - 1 if first else 0
            mine = ((self.g & bit) != 0).astype(jnp.int32)
            sent = lax.dynamic_index_in_dim(held, 1 - mine, axis, keepdims=False).astype(bf16)
            kept = lax.dynamic_index_in_dim(held, mine, axis, keepdims=False)
            got = self.around(sent, bit)
            left -= 1
            if left == 0:
                return sent, kept, got
            held = kept + got.astype(f32)

    def slot_blocks(self, held):
        half = held[0].shape[-2] // 2
        return [
            lax.dynamic_slice_in_dim(value, (j1 ^ (self.seq >> 1)) * half, half, value.ndim - 2).astype(bf16)
            for value in held for j1 in (0, 1)
        ]

    def slot_sends(self, blocks, slots):
        return [self.unslot(blocks[2 * i + j1], j1, j0) for i, j0 in enumerate(slots) for j1 in (0, 1)]

    def slot_total(self, got):
        return sum(v.astype(f32) for v in got)


def per_device(
    groups, tensor,
    inputs, segment, cotangent, norm_gain, weight_z, weight_x, weight_bc, weight_dt, conv_weight_x, conv_bias_x,
    conv_weight_bc, conv_bias_bc, step_bias, decay_log, skip_gain, gate_gain, weight_out,
):
    plan = Plan(groups, tensor, inputs.shape[0])
    shares = plan.shares
    length = inputs.shape[1]
    model = norm_gain.shape[0]
    width = conv_bias_x.shape[0]
    heads = step_bias.shape[0]
    wide = conv_bias_bc.shape[0]
    inner = width * tensor
    two = (0, 1)

    other = plan.send(segment, lambda g, c, t: (g, 1 - c, t))
    both_seg = jnp.where(plan.c == 0, jnp.concatenate([segment, other]), jnp.concatenate([other, segment]))
    seg = lax.dynamic_index_in_dim(both_seg, plan.seq, 0, keepdims=False)
    blocks = seg.reshape(length // SPAN, SPAN)
    ends = blocks[:, -1]
    starts = jnp.concatenate([jnp.full((1,), -1, jnp.int32), ends[:-1]])
    flags = [(blocks == starts[:, None]).reshape(length), (blocks == ends[:, None]).reshape(length)]
    flags += [jnp.concatenate([jnp.zeros((k,), bool), seg[k:] == seg[:-k]]) for k in (1, 2, 3)]
    flags += [jnp.concatenate([seg[k:] == seg[:-k], jnp.zeros((k,), bool)]) for k in (1, 2, 3)]
    aux = jnp.stack(flags, axis=1).astype(f32)
    seg_column, seg_row = seg[:, None], seg[None]
    head_row = jnp.zeros((1, width), f32)
    head_row = lax.dynamic_update_slice(head_row, jnp.concatenate([step_bias, decay_log, skip_gain])[None], (0, 0))
    exact = jnp.concatenate([conv_weight_x, conv_bias_x[None], gate_gain[None], head_row], axis=0)
    row_count = exact.shape[0]
    riders = [weight_dt.T.reshape(-1, width)] + thirds(exact)
    dt_rows = riders[0].shape[0]
    riders = jnp.concatenate(riders, axis=0)
    riders = jnp.pad(riders, ((0, -riders.shape[0] % 16), (0, 0)))
    mine_x = jnp.concatenate([plan.slice_of(weight_x), riders], axis=0)
    size = model // groups
    x_slots = [plan.slot(mine_x, j) for j in two]
    riders = [x_slots[j][size:] for j in two]
    mine_o = plan.slice_of(weight_out)
    mine = jnp.stack([plan.slice_of(weight_z), jnp.concatenate([mine_o[:, i : i + width] for i in range(0, model, width)], axis=0)])
    zo_slots = [plan.slot(tie(mine, *x_slots), j) for j in two]
    swapped_u, swapped_cot = plan.swap_for_sequence([inputs, cotangent])
    spread_x = [plan.spread(x_slots[j][:size], j == 0) for j in two]
    got_u = plan.to_sequence(tie(swapped_u, aux, seg_column, seg_row, spread_x[0][0][0], spread_x[1][0][0], *zo_slots))
    stacks, moves = [], []
    for j in two:
        found, offsets = spread_x[j]
        for stack, offs in zip(found, offsets):
            moves += [
                (len(stacks), (i,), slice(0, size), 0, size, off, slice(j * width, (j + 1) * width))
                for i, off in enumerate(offs)
            ]
            stacks.append(stack)
    w_x = assemble(moves, plan.g, stacks, (model, 2 * width))
    all_z = plan.spread(jnp.stack([zo_slots[j][0] for j in two]), True)
    all_o = plan.spread(jnp.stack([zo_slots[j][1] for j in two]), False)
    share_bc = lax.dynamic_slice_in_dim(weight_bc, plan.share * (wide // shares), wide // shares, 1)
    w_dt = [v[:dt_rows].reshape(heads, model) for v in riders]
    slots = [
        sum(v[dt_rows + i * row_count : dt_rows + (i + 1) * row_count].astype(f32) for i in (2, 1, 0)) for v in riders
    ]
    rows = jnp.concatenate(slots, axis=1)
    conv_w, conv_b, gain = rows[0:4], rows[4:5], rows[5:6]
    bias, log_rate, skip = (
        jnp.concatenate([v[6:7, i * heads : (i + 1) * heads] for v in slots], axis=1) for i in range(3)
    )
    w_dt = jnp.concatenate(w_dt, axis=0)
    rate, skip_lanes = -jnp.exp(log_rate), jnp.repeat(skip, HEAD, axis=1)
    where = jnp.stack([plan.share, (plan.g & plan.bits[-1]) // plan.bits[-1], plan.g & 1, plan.t])
    got_u = tie(
        got_u, w_x, all_z[0][0], all_o[0][0], share_bc, w_dt, conv_w, conv_b, gain, bias, rate, skip_lanes, where, swapped_cot
    )
    got_cot = plan.to_sequence(tie(swapped_cot, got_u))
    u_part_low = plan.pieces_of_sequence(got_u)
    u_part = u_part_low.astype(f32)
    scale_part = lax.rsqrt(jnp.mean(u_part * u_part, axis=-1, keepdims=True) + EPS)
    normed = lax.optimization_barrier(plan.gather_shares((u_part * scale_part * norm_gain).astype(bf16)))

    bc_pre = dot_nn(normed, weight_bc)
    common = (
        dot_nn(normed, w_x), bc_pre, dot_nt(normed, w_dt) + bias, rate, aux, seg_column, seg_row,
        conv_w, conv_b, conv_weight_bc, conv_bias_bc[None], skip_lanes,
    )
    y, entering, steps, cum_t = forward_scan(common)

    z_stacks, o_stacks = tie((all_z[0], all_o[0]), y)
    moves = [
        (n, (i, j), slice(0, size), 0, size, off, slice(j * width, (j + 1) * width))
        for n in two for i, off in enumerate(all_z[1][n]) for j in two
    ]
    w_z = assemble(moves, plan.g, z_stacks, (model, 2 * width))
    tall = width // groups
    moves = [
        (n, (i, j), slice(m * tall, (m + 1) * tall), j * width, tall, off, slice(m * width, (m + 1) * width))
        for n in two for i, off in enumerate(all_o[1][n]) for j in two for m in range(model // width)
    ]
    w_out = assemble(moves, plan.g, o_stacks, (2 * width, model))
    cot_part = plan.pieces_of_sequence(tie(got_cot, y))
    cot_parts = [cot_part] + [plan.across(cot_part, e) for e in range(1, shares)]
    stats, c_sent, c_kept = gate_step(shares, where, normed, w_z, y, w_out, gain, cot_parts)
    mixed, d_y, d_gate, grad_gain, sent_y, out_part = norm_step(
        shares, inner, where, normed, w_z, y, w_out, gain, plan.sum_shares(stats), cot_parts
    )
    rows_per = length // shares
    for e in range(1, shares):
        out_part = out_part.astype(f32) + plan.across(sent_y[(shares - 1 - e) * rows_per : (shares - e) * rows_per], e).astype(f32)
    out_low = (u_part_low.astype(f32) + out_part).astype(bf16)
    out_blocks = plan.blocks_back(out_low)
    got_out = plan.from_sequence(out_blocks)
    grad_gain = grad_gain[0]

    x_sent, x_kept = cut_step(groups, where, normed)
    sent_z = dot_nn(x_sent, d_gate).astype(bf16)
    sent_o = dot_nn(c_sent, mixed).astype(bf16)
    early_z = plan.first_send(sent_z, True)
    early_o = plan.first_send(sent_o, False)

    def slots_of(value):
        return [value[:, j * width : (j + 1) * width] for j in two]

    back = [backward_scan(common, 0, shares, where, steps, cum_t, y, tie(d_y, sent_z, sent_o, out_blocks), entering)]
    early_z, early_o = tie((early_z, early_o), back[0][1])
    next_z, held_z, late_z = plan.next_sums(dot_nn(x_kept, d_gate) + early_z.astype(f32), True)
    next_o, held_o, late_o = plan.next_sums(dot_nn(c_kept, mixed) + early_o.astype(f32), False)
    first = tie(back[0][1], next_z, next_o, got_out)
    sent_x = dot_nn(x_sent, first).astype(bf16)
    early_x = plan.first_send(sent_x, True)
    kept_x = dot_nn(x_kept, first)
    base = base_step(d_gate, w_z, first, w_x)
    late_z, late_o = tie((late_z, late_o), sent_x, kept_x, base)
    late_z = held_z + late_z.astype(f32)
    late_o = held_o + late_o.astype(f32)
    zo_blocks = plan.slot_blocks([jnp.stack(v) for v in zip(slots_of(late_z), slots_of(late_o))])
    back.append(backward_scan(common, 1, shares, where, steps, cum_t, y, tie(d_y, zo_blocks), entering, back[0][0]))
    zo_sums = plan.slot_sends(zo_blocks, two)
    u_parts = [u_part_low] + [plan.across(tie(u_part_low, y), e) for e in range(1, shares)]
    back[1] = tie(back[1], zo_sums, early_x)

    next_x, held_x, late_x = plan.next_sums(kept_x + tie(early_x, back[1][1]).astype(f32), True)
    d_bcs = [back[1][0][0]] + [plan.across(back[1][0][e], e) for e in range(1, shares)]
    sent_d, d_part, low_bc, grad_norm = last_step(
        shares, where, d_bcs, u_parts, back[1][1], (back[0][2], back[1][2]), tie(base, next_x, held_x), w_x, share_bc, w_dt
    )
    x0_blocks = plan.slot_blocks([held_x + tie(late_x, sent_d).astype(f32)])
    x0_sums = plan.slot_sends(x0_blocks, (0,))
    grad_norm = grad_norm[0]
    d_parts = [d_part] + [
        plan.across(sent_d[(shares - 1 - e) * rows_per : (shares - e) * rows_per], e) for e in range(1, shares)
    ]
    back_blocks = input_step(tensor, d_parts, tie(u_part_low, x0_blocks), norm_gain[None])
    got_back = plan.from_sequence(back_blocks)
    output, done = plan.pieces_of_batch(tie(got_out, back_blocks))

    rows = []
    for j in two:
        g_conv, g_heads = back[j][3], back[j][5]
        head_row = jnp.zeros((1, width), f32)
        g_skip = jnp.sum(g_conv[5].reshape(-1, HEAD), axis=1)
        head_row = lax.dynamic_update_slice(head_row, jnp.concatenate([g_heads[0], g_heads[1], g_skip])[None], (0, 0))
        rows.append(jnp.concatenate([g_conv[0:5], grad_gain[None, j * width : (j + 1) * width], head_row], axis=0))
    order = [rows[0], rows[1]]
    flip = (plan.seq & 1) != 0
    order = [jnp.where(flip, rows[1 - j], rows[j]) for j in two]
    shared = jnp.concatenate([grad_norm, (back[0][4] + back[1][4])[0:5].reshape(-1)])
    shared = jnp.pad(shared, (0, -shared.shape[0] % width)).reshape(-1, width)
    small = jnp.concatenate(order + [shared], axis=0)
    count = rows[0].shape[0]

    rest = jnp.concatenate([low_bc, back[0][2], back[1][2]], axis=1)
    size_r = model // groups
    sent_r, kept_r = (
        one_by_one(lax.dot_general(u, v, (((0,), (1,)), ((), ())), preferred_element_type=f32), size_r)
        for u, v in ((rest, x_sent), (tie(rest, done), x_kept))
    )
    pack = None
    for n, bit in enumerate(plan.bits):
        beside = side_by_side(sent_r.astype(bf16), width)
        message = jnp.concatenate([beside] + thirds(small), axis=0)
        pack = message if pack is None else pack
        got = plan.around(message, bit)
        if n == 0:
            got = tie(got, done)
        tall, lines = beside.shape[0], small.shape[0]
        kept_r = kept_r + one_by_one(got[:tall], size_r).astype(f32)
        small = small + sum(got[tall + i * lines : tall + (i + 1) * lines].astype(f32) for i in (2, 1, 0))
        if n + 1 < len(plan.bits):
            parts = groups >> (n + 1)
            held = kept_r.reshape(parts // 2, 2, kept_r.shape[0] // parts, size_r)
            mine = ((plan.g & plan.bits[n + 1]) != 0).astype(jnp.int32)
            sent_r, kept_r = (
                lax.dynamic_index_in_dim(held, v, 1, keepdims=False).reshape(-1, size_r) for v in (1 - mine, mine)
            )
    rest = kept_r

    final = tie(back[1][1], done)
    early_r = plan.first_send(dot_nn(x_sent, final).astype(bf16), True)
    kept_x1 = lax.optimization_barrier(dot_nn(x_kept, final))
    next_r, held_r, late_r = plan.next_sums(kept_x1 + tie(early_r, done).astype(f32), True)
    late_r = held_r + late_r.astype(f32)
    grad_z, grad_out = plan.slot_total(zo_sums)
    grad_out = grad_out.T
    input_grad = cotangent.astype(f32) + plan.pieces_of_batch(got_back)[0].astype(f32)

    beyond = wide // shares
    parts = [rest[:beyond]] + [
        jnp.where(flip, rest[beyond + (1 - j) * heads : beyond + (2 - j) * heads], rest[beyond + j * heads : beyond + (j + 1) * heads])
        for j in two
    ]
    rest = jnp.concatenate(parts, axis=0).astype(bf16)
    half = size_r // 2
    columns = rest.shape[0]
    rests, smalls = [], []
    for e in range(shares):
        rows_e = lax.dynamic_slice_in_dim(rest, ((plan.share ^ e) // plan.k) * half, half, 1)
        rests.append(plan.across(rows_e, e) if e else rows_e)
        smalls.append(plan.across(small, e) if e else small)
    rests = side_by_side(jnp.concatenate(order_by_xor(rests, plan.share), axis=0), width)
    smalls = order_by_xor(smalls, plan.share)
    shared = sum(v[2 * count :] for v in smalls)
    smalls = jnp.stack([
        jnp.concatenate([smalls[i // 2][(i % 2) * count : (i % 2 + 1) * count], shared], axis=0) for i in range(tensor)
    ])
    cells = rests.shape[0]
    rests = jnp.broadcast_to(rests[None], (tensor, cells, width))
    last = jnp.concatenate([rests] + thirds(smalls), axis=1)
    last = tie(last, next_r)
    x1_sums = plan.slot_sends(plan.slot_blocks([tie(late_r, last)]), (1,))
    last = lax.all_to_all(tie(last, got_back), "t", 0, 0, tiled=True).reshape(tensor, -1, width)
    grad_x = plan.slot_total(tie(x0_sums + x1_sums, last))
    rests = one_by_one(jnp.sum(last[:, :cells].astype(f32), axis=0), half)
    rests = [rests[i * columns : (i + 1) * columns] for i in range(shares)]
    grad_bc = jnp.concatenate([v[:beyond] for v in rests], axis=0).T
    dts = [v[beyond + j * heads : beyond + (j + 1) * heads] for v in rests for j in two]
    grad_dt = lax.dynamic_index_in_dim(jnp.stack(dts), plan.t, 0, keepdims=False).T
    g_conv, g_conv_bias, g_gain, g_step, g_decay, g_skip, g_norm, g_conv_bc, g_conv_bc_bias = finish_step(
        where, last, cells, model, wide, heads
    )
    return (
        output, input_grad, g_norm, grad_z, grad_x, grad_bc, grad_dt, g_conv, g_conv_bias, g_conv_bc, g_conv_bc_bias,
        g_step, g_decay, g_skip, g_gain, grad_out,
    )


def solution(mesh):
    data, tensor = mesh.shape["dp"], mesh.shape["tensor"]
    groups = data // 2
    fine = Mesh(mesh.devices.reshape(groups, 2, tensor), AXES)
    dp = ("g", "c")

    def step(*args):
        return per_device(groups, tensor, *args)

    return jax.shard_map(
        step,
        mesh=fine,
        in_specs=(
            P(dp, None, "t"), P(dp, None), P(dp, None, "t"), P(), P(None, "t"), P(None, "t"), P(), P(None, "t"),
            P(None, "t"), P("t"), P(), P(), P("t"), P("t"), P("t"), P("t"), P("t", None),
        ),
        out_specs=(
            P(dp, None, "t"), P(dp, None, "t"), P("t"), P(dp, "t"), P(dp, "t"), P(dp, None), P(dp, "t"),
            P(None, "t"), P("t"), P(), P(), P("t"), P("t"), P("t"), P("t"), P("t", dp),
        ),
        check_vma=False,
    )
```
